32 devices in a mesh: panel: 2 (over x), leaf: 16 (over z, y, core).
Axes of the slice: x: 2, y: 2, z: 4, core: 2. Of those that a mesh axis runs over, the one named last changes fastest.
Arguments:
- sources: bfloat16 [2, 832, 2, 1536], P('panel', 'leaf'), may hold values from -6 to 6
- transmission: float32 [2, 832, 128], P('panel', 'leaf')
- media: int32 [2, 832, 1], P('panel', 'leaf'), may hold values from 0 to 15; in each aligned block of 52 rows (0 to 51, 52 to 103, ..., all dimensions but the last counted through in order) at most 8 rows name the same one
- sep_code: int32 [2, 16], P('panel', 'leaf'), may hold values from 0 to 7
- leaf_factors: bfloat16 [16, 2, 768, 768], P('leaf'), may hold values from -0.15625 to 0.15625
- sep_factors: bfloat16 [2, 2, 384, 384], replicated, may hold values from -0.15625 to 0.15625
Outputs:
- solutions: bfloat16 [2, 832, 2, 1536], P('panel', 'leaf')
The draws below stay inside these ranges and needn't reach their ends.
Inputs may be any that keep to these rules, and one draw needn't show every extreme that they name: `media`: among the 52 leaves of one device (aligned blocks of rows) no library entry is named more than 8 times, a bound that some block reaches.
All inputs are finite; a program needn't handle non-finite values.
Results may differ from the reference program's by a relative error of at most 0.0065.
Values may be sent and summed in bfloat16 or wider, within the bound.
No kernel may reach another device: no remote copies, remote signals or barrier semaphores. Data moves between devices by JAX's collectives and lax.ppermute only.
A program may use at most 64 MiB of HBM per device.

```python
import math
import jax
import jax.numpy as jnp
import numpy as np
from jax import lax

LEAF_N = 768
SEP_N = 384
FRONT = 64
SEP_LIB = 2
SHOTS = 2
LEAVES_DEV = 52
LIB = 16
LEAVES = 832
CAP = 8
N_PANEL = 2
N_LEAF = 16


def draw_transmission(key, part):
    random_keys = jax.random.split(key, 5)
    shape_leaf = (1, LEAVES, FRONT)
    full_extent = (N_PANEL, LEAVES, FRONT)
    low_log = math.log(0.05 / N_PANEL)
    high_log = math.log(3.0)
    decay_rate = jnp.exp(jax.random.uniform(random_keys[0], shape_leaf, jnp.float32, low_log, high_log))
    panel_operator = jax.random.uniform(random_keys[1], full_extent, jnp.float32, 0.5, 2.0)
    impulse_train = jax.random.bernoulli(random_keys[2], 0.1, full_extent).astype(jnp.float32)
    impulse_penalty = jax.random.uniform(random_keys[3], full_extent, jnp.float32, 0.5, 0.8)
    field_amplitude = jnp.exp(-decay_rate * panel_operator) * (1.0 - impulse_train + impulse_train * impulse_penalty)
    phase = jax.random.uniform(random_keys[4], full_extent, jnp.float32, -math.pi, math.pi)
    return jnp.concatenate([field_amplitude * jnp.cos(phase), field_amplitude * jnp.sin(phase)], axis=-1)


def touch_ends(result, key, least, largest):
    longest = result.shape.index(max(result.shape))
    spots = []
    for shift in (0, 1):
        where = [jax.random.randint(jax.random.fold_in(key, axis), (), 0, length) for axis, length in enumerate(result.shape)]
        where[longest] = (where[longest] + shift) % result.shape[longest]
        spots.append(tuple(where))
    return result.at[spots[0]].set(least).at[spots[1]].set(largest)


def level_of(key, dims, cuts, low, high):
    loudness = 1.0
    for axis_at, blocks in cuts:
        draws = jax.random.uniform(jax.random.fold_in(jax.random.fold_in(key, 6), axis_at), (blocks,), jnp.float32, low / len(cuts), high / len(cuts))
        loudness = loudness * jnp.repeat(jnp.exp(draws), dims[axis_at] // blocks).reshape((-1,) + (1,) * (len(dims) - 1 - axis_at))
    return loudness


def deal_out(stream_key, own, number, rows, amount, top, reach, lean):
    sequence = jax.random.permutation(stream_key, amount)
    packed, usual = shares(amount, rows * top, reach, lean, True), shares(amount, rows * top, reach, lean, False)
    places = jnp.arange(amount)

    def named(tallies, turn):
        used = int((tallies > 0).sum())
        fixed = max(1, used // 4)
        moved = fixed + (places - fixed + turn * (used - fixed)) % max(1, amount - fixed)
        return jnp.zeros((amount,), jnp.int32).at[sequence[jnp.where(places < fixed, places, moved)]].set(jnp.asarray(tallies, jnp.int32))

    tallies = jnp.where(number % 4 == 0, named(packed, number // 4), named(usual, number - number // 4 - 1))
    mixed = jax.random.permutation(jax.random.fold_in(own, 3), amount)
    donor, sink = mixed[0:amount // 2 * 2:2], mixed[1:amount // 2 * 2:2]
    slack = jnp.minimum(tallies[donor] - 1, reach - tallies[sink]) // 2
    slack = jnp.where((donor == sequence[0]) | (sink == sequence[0]) | (tallies[sink] == 0), 0, jnp.maximum(slack, 0))
    moved = jax.random.randint(jax.random.fold_in(own, 4), (amount // 2,), 0, 1 << 20) % (slack + 1)
    tallies = tallies.at[donor].add(-moved).at[sink].add(moved)
    members = jnp.searchsorted(jnp.cumsum(tallies), jnp.arange(rows * top), side="right").astype(jnp.int32)
    grid = members.reshape(top, rows).T
    grid = grid[jax.random.permutation(jax.random.fold_in(own, 1), rows)]
    turn = jax.random.randint(jax.random.fold_in(own, 2), (rows, 1), 0, top)
    return jnp.take_along_axis(grid, (jnp.arange(top)[None, :] + turn) % top, axis=1)


def shares(count, total, bound, lean, full):
    weights = [(1 << 20) // math.isqrt(standing ** lean) + 1 for standing in range(1, count + 1)]
    largest = bound if full else min(bound, max(-(-total // count), total * weights[0] // sum(weights)))
    least = 1 if total - largest >= count - 1 else 0
    counts, spare = [largest] + [least] * (count - 1), total - largest - least * (count - 1)
    while spare > 0:
        movable = [i for i in range(1, count) if counts[i] < largest] or [i for i in range(1, count) if counts[i] < bound]
        pool, budget = sum([weights[i] for i in movable]), spare
        for i in movable:
            addition = min(bound - counts[i], max(1, budget * weights[i] // pool), spare)
            counts[i] = counts[i] + addition
            spare = spare - addition
    return np.array(counts)


def gaussian(own_key, dims, deviation, reach, shards=(), held_as=jnp.bfloat16):
    loudness = level_of(own_key, dims, shards, -0.22, 0.18) if shards else 1.0
    array = jax.random.normal(own_key, dims, jnp.float32) * deviation * loudness
    return jnp.minimum(jnp.maximum(array, -reach), reach).astype(held_as)


def setup_inputs(seed: int = 0) -> dict:
    streams_of = jax.random.split(jax.random.key(seed), 7)
    sources = gaussian(streams_of[0], (N_PANEL, LEAVES, SHOTS, 2 * LEAF_N), 1.0, 6.0, ((0, 2), (1, 16)))
    transmission = draw_transmission(jax.random.fold_in(streams_of[6], 71), 0)
    media_keys = jax.random.split(jax.random.fold_in(streams_of[2], 1), N_PANEL * LEAVES // LEAVES_DEV)
    media_turns = jax.random.permutation(jax.random.fold_in(streams_of[2], 3), N_PANEL * LEAVES // LEAVES_DEV)
    media = jax.vmap(lambda own, number: deal_out(jax.random.fold_in(streams_of[2], 2), own, number, LEAVES_DEV, LIB, 1, CAP, 1))(media_keys, media_turns).reshape((N_PANEL, LEAVES, 1))
    sep_code = touch_ends(jax.random.randint(streams_of[3], (N_PANEL, N_LEAF), 0, 8), jax.random.fold_in(streams_of[3], 1), 0, 7).astype(jnp.int32)
    leaf_factors = gaussian(streams_of[4], (LIB, 2, LEAF_N, LEAF_N), (2 * LEAF_N) ** -0.5, 0.15625, ((0, 16),))
    sep_factors = gaussian(streams_of[5], (SEP_LIB, 2, SEP_N, SEP_N), (4 * SEP_N) ** -0.5, 0.15625)
    return dict(sources=sources, transmission=transmission, media=media, sep_code=sep_code, leaf_factors=leaf_factors, sep_factors=sep_factors)


def complex_times(left, right, half):
    left_re, left_im = (left[..., :half], left[..., half:])
    right_re, right_im = (right[..., :half], right[..., half:])
    return jnp.concatenate([left_re * right_re - left_im * right_im, left_re * right_im + left_im * right_re], axis=-1)

def block_matrix(pair):
    real_part, imag_part = (pair[0], pair[1])
    upper = jnp.concatenate([real_part, imag_part], axis=1)
    lower = jnp.concatenate([-imag_part, real_part], axis=1)
    return jnp.concatenate([upper, lower], axis=0)

def face_rows(source, width, front):
    return jnp.concatenate([source[..., width - front:width], source[..., 2 * width - front:]], axis=-1)

def lift_face(incoming, width, front):
    gap = jnp.zeros(incoming.shape[:-1] + (width - front,), jnp.float32)
    return jnp.concatenate([gap, incoming[..., :front], gap, incoming[..., front:]], axis=-1)

def lift_top(values, width, sep):
    gap = jnp.zeros(values.shape[:-1] + (width - sep,), jnp.float32)
    return jnp.concatenate([values[..., :sep], gap, values[..., sep:], gap], axis=-1)

def trace_rows(solved, width, sep):
    return jnp.concatenate([solved[..., :sep], solved[..., width:width + sep]], axis=-1)

def reference(sources, transmission, media, sep_code, leaf_factors, sep_factors):
    face = face_rows(sources, LEAF_N, FRONT).astype(jnp.float32)

    def sweep_step(incoming, pieces):
        tau, front_src = pieces
        return (complex_times(tau[:, None, :], incoming + front_src, FRONT), incoming)
    start = jnp.zeros((LEAVES, SHOTS, 2 * FRONT), jnp.float32)
    _, arriving = lax.scan(sweep_step, start, (transmission, face))
    leaf_big = jax.vmap(block_matrix)(leaf_factors)
    sep_big = jax.vmap(block_matrix)(sep_factors)
    levels = N_LEAF.bit_length() - 1

    def one_panel(pieces):
        source, incoming, kinds, codes = pieces
        rhs = (source.astype(jnp.float32) + lift_face(incoming, LEAF_N, FRONT)).astype(jnp.bfloat16)

        def one_leaf(item):
            rows, kind = item
            return jnp.dot(rows, leaf_big[kind], preferred_element_type=jnp.float32).astype(jnp.bfloat16)
        solved = lax.map(one_leaf, (rhs, kinds[:, 0]))
        traces = trace_rows(solved.astype(jnp.float32), LEAF_N, SEP_N)
        traces = traces.reshape(N_LEAF, LEAVES_DEV, SHOTS, 2 * SEP_N).sum(axis=1)
        sep_sol = jnp.zeros((1, SHOTS, 2 * SEP_N), jnp.float32)
        for level in reversed(range(levels)):
            span = 2 ** (level + 1)
            nodes = N_LEAF // span
            block_sum = traces.reshape(nodes, span, SHOTS, 2 * SEP_N).sum(axis=1) * (1.0 / math.sqrt(LEAVES_DEV * span))
            block_code = codes.reshape(nodes, span).sum(axis=1) % SEP_LIB
            parent = jnp.repeat(sep_sol, nodes // sep_sol.shape[0], axis=0)
            operand = (block_sum - parent).astype(jnp.bfloat16)
            sep_sol = jnp.einsum('nsc,ncd->nsd', operand.astype(jnp.float32), sep_big[block_code].astype(jnp.float32))
        per_position = jnp.repeat(sep_sol, 2, axis=0)
        per_leaf = jnp.repeat(per_position, LEAVES_DEV, axis=0)
        return (solved.astype(jnp.float32) - lift_top(per_leaf, LEAF_N, SEP_N)).astype(jnp.bfloat16)
    return lax.map(one_panel, (sources, arriving, media, sep_code))
```

```python
import functools
import math

import jax
import jax.numpy as jnp
from jax import lax
from jax.experimental import pallas as pl
from jax.experimental.pallas import tpu as pltpu
from jax.sharding import PartitionSpec as P

F32 = jnp.float32
BF16 = jnp.bfloat16
VMEM = pltpu.VMEM


def from_behind(value, axis):
    count = lax.axis_size(axis)
    return lax.ppermute(value, axis, [(at, at + 1) for at in range(count - 1)])


def from_partner(value, axis, bit):
    pairs = [(at, at ^ (1 << bit)) for at in range(lax.axis_size(axis))]
    return lax.ppermute(value, axis, pairs)


def dot(left, right):
    return jnp.dot(left, right, preferred_element_type=F32)


def slot_of(kinds_ref, shots, capacity):
    kinds = kinds_ref[...]
    count = kinds.shape[1]
    before = lax.broadcasted_iota(jnp.int32, (count, count), 0)
    after = lax.broadcasted_iota(jnp.int32, (count, count), 1)
    across = jnp.broadcast_to(kinds, (count, count))
    down_kinds = jnp.sum(jnp.where(before == after, across, 0), axis=1, keepdims=True)
    down = jnp.broadcast_to(down_kinds, (count, count))
    same = (across == down) & (before % shots == after % shots)
    rank_row = jnp.sum((same & (before < after)).astype(jnp.int32), axis=0, keepdims=True)
    rank_col = jnp.sum((same & (after < before)).astype(jnp.int32), axis=1, keepdims=True)
    shot_row = lax.broadcasted_iota(jnp.int32, (1, count), 1) % shots
    shot_col = lax.broadcasted_iota(jnp.int32, (count, 1), 0) % shots
    row = (kinds * shots + shot_row) * capacity + rank_row
    col = (down_kinds * shots + shot_col) * capacity + rank_col
    return row, col


def dispatch_kernel(shots, capacity, front, kinds_ref, rows_ref, arriving_ref, send_ref, rhs_ref):
    width2 = rows_ref.shape[1]
    leaf_n = width2 // 2
    rhs_ref[...] = rows_ref[...]
    for part in range(2):
        face = pl.ds((part + 1) * leaf_n - 2 * front, 2 * front)
        incoming = arriving_ref[...]
        place = lax.broadcasted_iota(jnp.int32, incoming.shape, 1)
        if part == 0:
            incoming = pltpu.roll(incoming, front, 1)
        incoming = jnp.where(place >= front, incoming, 0.0)
        rhs_ref[:, face] = (rows_ref[:, face].astype(F32) + incoming).astype(BF16)
    row, _ = slot_of(kinds_ref, shots, capacity)
    slots = send_ref.shape[0]
    place = lax.broadcasted_iota(jnp.int32, (slots, row.shape[1]), 0)
    pick = (place == row).astype(F32).astype(BF16)
    send_ref[...] = dot(pick, rhs_ref[...]).astype(BF16)


def leaf_kernel(capacity, sep_n, arrived_ref, factor_ref, solved_ref, sums_ref):
    leaf_n = factor_ref.shape[1]
    real, imag = arrived_ref[:, :leaf_n], arrived_ref[:, leaf_n:]
    factor_re, factor_im = factor_ref[0], factor_ref[1]
    solved_ref[:, :leaf_n] = (dot(real, factor_re) - dot(imag, factor_im)).astype(BF16)
    solved_ref[:, leaf_n:] = (dot(real, factor_im) + dot(imag, factor_re)).astype(BF16)
    groups, slots = sums_ref.shape[0], solved_ref.shape[0]
    group = lax.broadcasted_iota(jnp.int32, (groups, slots), 0)
    place = lax.broadcasted_iota(jnp.int32, (groups, slots), 1)
    member = (place // capacity == group).astype(F32).astype(BF16)
    sums_ref[:, :sep_n] = dot(member, solved_ref[:, :sep_n])
    sums_ref[:, sep_n:] = dot(member, solved_ref[:, leaf_n : leaf_n + sep_n])


def tree_kernel(scales, codes_ref, sums_ref, factors_ref, out_ref):
    sep_n = factors_ref.shape[2]
    above = jnp.zeros(out_ref.shape, F32)
    for level in reversed(range(len(scales))):
        operand = (sums_ref[level] * scales[level] - above).astype(BF16)
        real, imag = operand[:, :sep_n], operand[:, sep_n:]
        factor = factors_ref[codes_ref[level]]
        above = jnp.concatenate(
            [
                dot(real, factor[0]) - dot(imag, factor[1]),
                dot(real, factor[1]) + dot(imag, factor[0]),
            ],
            axis=1,
        )
    out_ref[...] = above


def result_kernel(shots, capacity, kinds_ref, back_ref, above_ref, out_ref):
    count, width2 = out_ref.shape
    leaf_n = width2 // 2
    sep_n = above_ref.shape[1] // 2
    _, col = slot_of(kinds_ref, shots, capacity)
    place = lax.broadcasted_iota(jnp.int32, (count, back_ref.shape[0]), 1)
    pick = (place == col).astype(F32).astype(BF16)
    solved = dot(pick, back_ref[...])
    shot = lax.broadcasted_iota(jnp.int32, (count, 2 * sep_n), 0) % shots
    lifted = jnp.zeros((count, 2 * sep_n), F32)
    for at in range(shots):
        lifted = jnp.where(shot == at, above_ref[at : at + 1, :], lifted)
    for part in range(2):
        start = part * leaf_n
        top = solved[:, start : start + sep_n] - lifted[:, part * sep_n : (part + 1) * sep_n]
        out_ref[:, start : start + sep_n] = top.astype(BF16)
        out_ref[:, start + sep_n : start + leaf_n] = solved[:, start + sep_n : start + leaf_n].astype(BF16)


def call(kernel, out_shape, args, smem=(), scratch=(), limit=32):
    return pl.pallas_call(
        kernel,
        out_shape=out_shape,
        in_specs=[
            pl.BlockSpec(memory_space=pltpu.SMEM if at in smem else VMEM) for at in range(len(args))
        ],
        out_specs=jax.tree.map(lambda _: pl.BlockSpec(memory_space=VMEM), out_shape),
        scratch_shapes=list(scratch),
        compiler_params=pltpu.CompilerParams(vmem_limit_bytes=limit * 2**20),
    )(*args)


def node_sums(own_sums, code, levels):
    me = lax.axis_index("leaf")
    positions = own_sums.shape[0]
    mine = jnp.arange(positions, dtype=jnp.int32) == me
    codes = jnp.where(mine, code, 0).astype(F32)
    codes = jnp.broadcast_to(codes[:, None, None], own_sums.shape[:2] + (128,))
    share = jnp.concatenate([own_sums, codes], axis=-1)
    shares = []
    for _ in range(levels):
        share = share.reshape((share.shape[0] // 2, 2) + share.shape[1:]).sum(axis=1)
        shares.append(share)
    for bit in range(levels):
        high = (me >> bit) & 1
        keep, send = [], []
        for level, share in enumerate(shares):
            if level < bit:
                pairs = share.reshape((share.shape[0] // 2, 2) + share.shape[1:])
                keep.append(jnp.where(high == 1, pairs[:, 1], pairs[:, 0]))
                send.append(jnp.where(high == 1, pairs[:, 0], pairs[:, 1]))
            else:
                keep.append(share)
                send.append(share)
        arrived = from_partner(jnp.concatenate(send, axis=0), "leaf", bit)
        ends = [0]
        for share in keep:
            ends.append(ends[-1] + share.shape[0])
        shares = [share + arrived[a:b] for share, a, b in zip(keep, ends[:-1], ends[1:])]
    path = jnp.concatenate(shares, axis=0)
    return path


def on_device(sources, transmission, media, sep_code, leaf_factors, sep_factors):
    leaves, shots, width2 = sources.shape[1:]
    leaf_n = width2 // 2
    front = transmission.shape[2] // 2
    sep_n = sep_factors.shape[2]
    sep_lib = sep_factors.shape[0]
    nleaf = lax.axis_size("leaf")
    levels = nleaf.bit_length() - 1
    capacity = max(2, leaves * 5 // (nleaf * 2))
    slots = nleaf * capacity * shots
    source, tau = sources[0], transmission[0][:, None, :]
    tau_re, tau_im = tau[..., :front], tau[..., front:]
    face_re = source[..., leaf_n - front : leaf_n].astype(F32)
    face_im = source[..., 2 * leaf_n - front :].astype(F32)
    arriving = jnp.zeros((leaves, shots, 2 * front), F32)
    for _ in range(lax.axis_size("panel") - 1):
        real, imag = arriving[..., :front] + face_re, arriving[..., front:] + face_im
        leaving = jnp.concatenate([tau_re * real - tau_im * imag, tau_re * imag + tau_im * real], axis=-1)
        arriving = from_behind(leaving, "panel")
    kinds = jnp.repeat(media[0, :, 0], shots)[None, :]
    rows = leaves * shots
    send = call(
        functools.partial(dispatch_kernel, shots, capacity, front),
        jax.ShapeDtypeStruct((slots, width2), BF16),
        (kinds, source.reshape(rows, width2), arriving.reshape(rows, 2 * front)),
        scratch=[pltpu.VMEM((rows, width2), BF16)],
    )
    split = (nleaf, capacity * shots, width2)
    arrived = lax.all_to_all(send.reshape(split), "leaf", split_axis=0, concat_axis=0, tiled=True)
    solved, sums = call(
        functools.partial(leaf_kernel, capacity, sep_n),
        (
            jax.ShapeDtypeStruct((slots, width2), BF16),
            jax.ShapeDtypeStruct((nleaf * shots, 2 * sep_n), F32),
        ),
        (arrived.reshape(slots, width2), leaf_factors[0]),
    )
    back = lax.all_to_all(solved.reshape(split), "leaf", split_axis=0, concat_axis=0, tiled=True)
    path = node_sums(sums.reshape(nleaf, shots, 2 * sep_n), sep_code[0, 0], levels)
    codes = path[:, 0, 2 * sep_n].astype(jnp.int32) % sep_lib
    scales = [1.0 / math.sqrt(leaves * 2 ** (level + 1)) for level in range(levels)]
    above = call(
        functools.partial(tree_kernel, scales),
        jax.ShapeDtypeStruct((shots, 2 * sep_n), F32),
        (codes, path[..., : 2 * sep_n], sep_factors),
        smem=(0,),
    )
    result = call(
        functools.partial(result_kernel, shots, capacity),
        jax.ShapeDtypeStruct((rows, width2), BF16),
        (kinds, back.reshape(slots, width2), above),
    )
    return result.reshape(1, leaves, shots, width2)


def solution(mesh):
    return jax.shard_map(
        on_device,
        mesh=mesh,
        in_specs=(
            P("panel", "leaf", None, None),
            P("panel", "leaf", None),
            P("panel", "leaf", None),
            P("panel", "leaf"),
            P("leaf", None, None, None),
            P(),
        ),
        out_specs=P("panel", "leaf", None, None),
        check_vma=False,
    )
```

```python
import functools
import math

import jax
import jax.numpy as jnp
from jax import lax
from jax.experimental import pallas as pl
from jax.experimental.pallas import tpu as pltpu
from jax.sharding import PartitionSpec as P

F32 = jnp.float32
BF16 = jnp.bfloat16
VMEM = pltpu.VMEM
LANES = 128


def from_behind(value, axis):
    count = lax.axis_size(axis)
    return lax.ppermute(value, axis, [(at, at + 1) for at in range(count - 1)])


def dot(left, right):
    return jnp.dot(left, right, preferred_element_type=F32)


def slot_of(kinds_ref, shots, capacity):
    kinds = kinds_ref[...]
    count = kinds.shape[1]
    before = lax.broadcasted_iota(jnp.int32, (count, count), 0)
    after = lax.broadcasted_iota(jnp.int32, (count, count), 1)
    across = jnp.broadcast_to(kinds, (count, count))
    down_kinds = jnp.sum(jnp.where(before == after, across, 0), axis=1, keepdims=True)
    down = jnp.broadcast_to(down_kinds, (count, count))
    same = (across == down) & (before % shots == after % shots)
    rank_row = jnp.sum((same & (before < after)).astype(jnp.int32), axis=0, keepdims=True)
    rank_col = jnp.sum((same & (after < before)).astype(jnp.int32), axis=1, keepdims=True)
    shot_row = lax.broadcasted_iota(jnp.int32, (1, count), 1) % shots
    shot_col = lax.broadcasted_iota(jnp.int32, (count, 1), 0) % shots
    row = (kinds * shots + shot_row) * capacity + rank_row
    col = (down_kinds * shots + shot_col) * capacity + rank_col
    return row, col


def dispatch_kernel(shots, capacity, front, kinds_ref, rows_ref, arriving_ref, out_ref, rhs_ref, send_ref, sems):
    width2 = rows_ref.shape[1]
    leaf_n = width2 // 2
    rhs_ref[...] = rows_ref[...]
    for part in range(2):
        face = pl.ds((part + 1) * leaf_n - 2 * front, 2 * front)
        incoming = arriving_ref[...]
        place = lax.broadcasted_iota(jnp.int32, incoming.shape, 1)
        if part == 0:
            incoming = pltpu.roll(incoming, front, 1)
        incoming = jnp.where(place >= front, incoming, 0.0)
        rhs_ref[:, face] = (rows_ref[:, face].astype(F32) + incoming).astype(BF16)
    row, _ = slot_of(kinds_ref, shots, capacity)
    slots = send_ref.shape[0]
    place = lax.broadcasted_iota(jnp.int32, (slots, row.shape[1]), 0)
    pick = (place == row).astype(F32).astype(BF16)
    copies = []
    for part in range(2):
        columns = pl.ds(part * leaf_n, leaf_n)
        send_ref[:, columns] = dot(pick, rhs_ref[:, columns]).astype(BF16)
        copies.append(pltpu.make_async_copy(send_ref.at[:, columns], out_ref.at[:, columns], sems.at[part]))
        copies[part].start()
    for copy in copies:
        copy.wait()


def leaf_kernel(capacity, shots, levels, sep_n, place_ref, arrived_ref, factor_ref, out_ref, solved_ref, sems):
    leaf_n = factor_ref.shape[1]
    block = capacity * shots
    slots = solved_ref.shape[0]
    real, imag = arrived_ref[:, :leaf_n], arrived_ref[:, leaf_n:]
    factor_re, factor_im = factor_ref[0], factor_ref[1]

    def leave(part, start, size):
        columns = pl.ds(start, size)
        copy = pltpu.make_async_copy(solved_ref.at[:, columns], out_ref.at[:, columns], sems.at[part])
        copy.start()
        return copy

    solved_ref[:, :leaf_n] = (dot(real, factor_re) - dot(imag, factor_im)).astype(BF16)
    copies = [leave(0, 0, leaf_n)]
    solved_ref[:, leaf_n : 2 * leaf_n] = (dot(real, factor_im) + dot(imag, factor_re)).astype(BF16)
    copies.append(leave(1, leaf_n, leaf_n))
    row = lax.broadcasted_iota(jnp.int32, (slots, slots), 0)
    col = lax.broadcasted_iota(jnp.int32, (slots, slots), 1)
    col_shot = col // capacity % shots
    first = 2 * leaf_n
    for start in range(0, 2 * levels * shots, block):
        entry = start + row % block
        level = entry // shots % levels
        near = (row // block) >> (level + 1) == (col // block) >> (level + 1)
        member = near & (entry % shots == col_shot) & (entry < 2 * levels * shots)
        total = jnp.zeros((slots, sep_n), F32)
        for part in range(2):
            pick = (member & (entry // (levels * shots) == part)).astype(F32).astype(BF16)
            total = total + dot(pick, solved_ref[:, part * leaf_n : part * leaf_n + sep_n])
        solved_ref[:, first : first + sep_n] = total.astype(BF16)
        first = first + sep_n
    row = lax.broadcasted_iota(jnp.int32, (slots, LANES), 0)
    level = lax.broadcasted_iota(jnp.int32, (slots, LANES), 1)
    me, code = place_ref[0], place_ref[1]
    near = ((row // block) >> (level + 1) == me >> (level + 1)) & (level < levels)
    solved_ref[:, first:] = jnp.where(near, code, 0).astype(F32).astype(BF16)
    copies.append(leave(2, 2 * leaf_n, solved_ref.shape[1] - 2 * leaf_n))
    for copy in copies:
        copy.wait()


def result_kernel(shots, capacity, scales, kinds_ref, back_ref, factors_ref, out_ref):
    count, width2 = out_ref.shape
    leaf_n = width2 // 2
    sep_lib, sep_n = factors_ref.shape[0], factors_ref.shape[2]
    slots, block, levels = back_ref.shape[0], capacity * shots, len(scales)
    row = lax.broadcasted_iota(jnp.int32, (block, slots), 0)
    col = lax.broadcasted_iota(jnp.int32, (block, slots), 1)
    same = (col % block == row).astype(F32).astype(BF16)
    sums = dot(same, back_ref[:, width2:])
    codes = sums[0:1, sums.shape[1] - LANES :]
    lane = lax.broadcasted_iota(jnp.int32, codes.shape, 1)
    codes = [jnp.sum(jnp.where(lane == level, codes, 0.0)).astype(jnp.int32) % sep_lib for level in range(levels)]

    def path_sum(part, level):
        entry = (part * levels + level) * shots
        rows, cols = entry % block, entry // block * sep_n
        return sums[rows : rows + shots, cols : cols + sep_n]

    above = jnp.zeros((2 * shots, sep_n), F32)
    for level in reversed(range(levels)):
        path = jnp.concatenate([path_sum(0, level), path_sum(1, level)], axis=0)
        operand = (path * scales[level] - above).astype(BF16)
        factor = factors_ref[codes[level]]
        by_re, by_im = dot(operand, factor[0]), dot(operand, factor[1])
        above = jnp.concatenate([by_re[:shots] - by_im[shots:], by_im[:shots] + by_re[shots:]], axis=0)
    _, col = slot_of(kinds_ref, shots, capacity)
    place = lax.broadcasted_iota(jnp.int32, (count, slots), 1)
    pick = (place == col).astype(F32).astype(BF16)
    shot = lax.broadcasted_iota(jnp.int32, (count, sep_n), 0) % shots
    for part in range(2):
        start = part * leaf_n
        solved = dot(pick, back_ref[:, start : start + leaf_n])
        lifted = jnp.zeros((count, sep_n), F32)
        for at in range(shots):
            here = part * shots + at
            lifted = jnp.where(shot == at, above[here : here + 1], lifted)
        out_ref[:, start : start + sep_n] = (solved[:, :sep_n] - lifted).astype(BF16)
        out_ref[:, start + sep_n : start + leaf_n] = solved[:, sep_n:].astype(BF16)


def face_kernel(front, source_ref, tau_ref, out_ref):
    leaf_n = source_ref.shape[2] // 2
    both = 2 * front
    face_re = source_ref[:, :, leaf_n - both : leaf_n].astype(F32)
    face_im = source_ref[:, :, 2 * leaf_n - both :].astype(F32)
    tau = tau_ref[...]
    first = lax.broadcasted_iota(jnp.int32, tau.shape, 2) < front
    turned = pltpu.roll(tau, front, 2)
    by_same, by_other = jnp.where(first, tau, turned), jnp.where(first, -turned, tau)
    first = lax.broadcasted_iota(jnp.int32, face_re.shape, 2) < front
    face = jnp.where(first, pltpu.roll(face_re, front, 2), face_im)
    other = jnp.where(first, pltpu.roll(face_im, front, 2), face_re)
    out_ref[...] = by_same * face + by_other * other


def call(kernel, out_shape, args, smem=(), scratch=(), to_hbm=False, limit=32):
    return pl.pallas_call(
        kernel,
        out_shape=out_shape,
        in_specs=[
            pl.BlockSpec(memory_space=pltpu.SMEM if at in smem else VMEM) for at in range(len(args))
        ],
        out_specs=pl.BlockSpec(memory_space=pl.ANY if to_hbm else VMEM),
        scratch_shapes=list(scratch),
        compiler_params=pltpu.CompilerParams(vmem_limit_bytes=limit * 2**20),
    )(*args)


def on_device(sources, transmission, media, sep_code, leaf_factors, sep_factors):
    leaves, shots, width2 = sources.shape[1:]
    leaf_n = width2 // 2
    front = transmission.shape[2] // 2
    sep_n = sep_factors.shape[2]
    nleaf = lax.axis_size("leaf")
    levels = nleaf.bit_length() - 1
    capacity = max(2, leaves * 5 // (nleaf * 2))
    block = capacity * shots
    slots = nleaf * block
    source, tau = sources[0], transmission[0][:, None, :]
    leaving = call(
        functools.partial(face_kernel, front),
        jax.ShapeDtypeStruct((leaves, shots, 2 * front), F32),
        (source, tau),
    )
    arriving = from_behind(leaving, "panel")
    tau_re, tau_im = tau[..., :front], tau[..., front:]
    for _ in range(lax.axis_size("panel") - 2):
        real = arriving[..., :front] + source[..., leaf_n - front : leaf_n].astype(F32)
        imag = arriving[..., front:] + source[..., 2 * leaf_n - front :].astype(F32)
        leaving = jnp.concatenate([tau_re * real - tau_im * imag, tau_re * imag + tau_im * real], axis=-1)
        arriving = from_behind(leaving, "panel")
    kinds = jnp.repeat(media[0, :, 0], shots)[None, :]
    rows = leaves * shots
    send = call(
        functools.partial(dispatch_kernel, shots, capacity, front),
        jax.ShapeDtypeStruct((slots, width2), BF16),
        (kinds, source.reshape(rows, width2), arriving.reshape(rows, 2 * front)),
        scratch=[VMEM((rows, width2), BF16), VMEM((slots, width2), BF16), pltpu.SemaphoreType.DMA((2,))],
        to_hbm=True,
    )
    arrived = lax.all_to_all(send.reshape(nleaf, block, width2), "leaf", split_axis=0, concat_axis=0, tiled=True)
    wide = width2 + -(-2 * levels // capacity) * sep_n + LANES
    place = jnp.stack([lax.axis_index("leaf"), sep_code[0, 0]])
    solved = call(
        functools.partial(leaf_kernel, capacity, shots, levels, sep_n),
        jax.ShapeDtypeStruct((slots, wide), BF16),
        (place, arrived.reshape(slots, width2), leaf_factors[0]),
        smem=(0,),
        scratch=[VMEM((slots, wide), BF16), pltpu.SemaphoreType.DMA((3,))],
        to_hbm=True,
    )
    back = lax.all_to_all(solved.reshape(nleaf, block, wide), "leaf", split_axis=0, concat_axis=0, tiled=True)
    scales = [1.0 / math.sqrt(leaves * 2 ** (level + 1)) for level in range(levels)]
    result = call(
        functools.partial(result_kernel, shots, capacity, scales),
        jax.ShapeDtypeStruct((rows, width2), BF16),
        (kinds, back.reshape(slots, wide), sep_factors),
    )
    return result.reshape(1, leaves, shots, width2)


def solution(mesh):
    return jax.shard_map(
        on_device,
        mesh=mesh,
        in_specs=(
            P("panel", "leaf", None, None),
            P("panel", "leaf", None),
            P("panel", "leaf", None),
            P("panel", "leaf"),
            P("leaf", None, None, None),
            P(),
        ),
        out_specs=P("panel", "leaf", None, None),
        check_vma=False,
    )
```

```python
import functools
import math

import jax
import jax.numpy as jnp
from jax import lax
from jax.experimental import pallas as pl
from jax.experimental.pallas import tpu as pltpu
from jax.sharding import PartitionSpec as P

F32 = jnp.float32
BF16 = jnp.bfloat16
VMEM = pltpu.VMEM
LANES = 128


def from_behind(value, axis):
    count = lax.axis_size(axis)
    return lax.ppermute(value, axis, [(at, at + 1) for at in range(count - 1)])


def exchange(value, distance):
    pairs = [(at, at ^ distance) for at in range(lax.axis_size("leaf"))]
    return lax.ppermute(value, "leaf", pairs)


def after(value, *others):
    return lax.optimization_barrier((value, *others))[0]


def dot(left, right):
    return jnp.dot(left, right, preferred_element_type=F32)


def one_hot(mask):
    return mask.astype(F32).astype(BF16)


def slot_of(place_ref, kinds_ref, shots, capacity):
    kinds = kinds_ref[...]
    count = kinds.shape[1]
    before = lax.broadcasted_iota(jnp.int32, (count, count), 0)
    later = lax.broadcasted_iota(jnp.int32, (count, count), 1)
    across = jnp.broadcast_to(kinds, (count, count))
    kinds_down = jnp.sum(jnp.where(before == later, across, 0), axis=1, keepdims=True)
    down = jnp.broadcast_to(kinds_down, (count, count))
    same = (across == down) & (before % shots == later % shots)
    rank_row = jnp.sum((same & (before < later)).astype(jnp.int32), axis=0, keepdims=True)
    rank_col = jnp.sum((same & (later < before)).astype(jnp.int32), axis=1, keepdims=True)
    shot_row = lax.broadcasted_iota(jnp.int32, (1, count), 1) % shots
    shot_col = lax.broadcasted_iota(jnp.int32, (count, 1), 0) % shots
    me = place_ref[0]
    row = ((kinds ^ me) * shots + shot_row) * capacity + rank_row
    col = ((kinds_down ^ me) * shots + shot_col) * capacity + rank_col
    return row, col


def face_kernel(front, source_ref, tau_ref, out_ref, re_ref, im_ref, through_ref, sems):
    leaf_n = source_ref.shape[2] // 2
    both = 2 * front
    copies = [
        pltpu.make_async_copy(source_ref.at[:, :, pl.ds(leaf_n - both, both)], re_ref, sems.at[0]),
        pltpu.make_async_copy(source_ref.at[:, :, pl.ds(2 * leaf_n - both, both)], im_ref, sems.at[1]),
        pltpu.make_async_copy(tau_ref, through_ref, sems.at[2]),
    ]
    for copy in copies:
        copy.start()
    for copy in copies:
        copy.wait()
    face_re, face_im = re_ref[...].astype(F32), im_ref[...].astype(F32)
    tau = through_ref[...]
    first = lax.broadcasted_iota(jnp.int32, tau.shape, 2) < front
    turned = pltpu.roll(tau, front, 2)
    by_same, by_other = jnp.where(first, tau, turned), jnp.where(first, -turned, tau)
    first = lax.broadcasted_iota(jnp.int32, face_re.shape, 2) < front
    face = jnp.where(first, pltpu.roll(face_re, front, 2), face_im)
    other = jnp.where(first, pltpu.roll(face_im, front, 2), face_re)
    out_ref[...] = by_same * face + by_other * other


def dispatch_kernel(shots, capacity, front, place_ref, kinds_ref, rows_ref, arriving_ref, *refs):
    out_refs, rhs_ref = refs[:-1], refs[-1]
    leaf_n = rows_ref.shape[1] // 2
    rhs_ref[...] = rows_ref[...]
    for part in range(2):
        face = pl.ds((part + 1) * leaf_n - 2 * front, 2 * front)
        incoming = arriving_ref[...]
        lane = lax.broadcasted_iota(jnp.int32, incoming.shape, 1)
        if part == 0:
            incoming = pltpu.roll(incoming, front, 1)
        incoming = jnp.where(lane >= front, incoming, 0.0)
        rhs_ref[:, face] = (rows_ref[:, face].astype(F32) + incoming).astype(BF16)
    row, _ = slot_of(place_ref, kinds_ref, shots, capacity)
    size = out_refs[0].shape[0]
    slots = size * len(out_refs)
    place = lax.broadcasted_iota(jnp.int32, (slots, row.shape[1]), 0)
    send = dot(one_hot(place == row), rhs_ref[...]).astype(BF16)
    for at, out_ref in enumerate(out_refs):
        out_ref[...] = send[at * size : (at + 1) * size]


def leaf_kernel(count, capacity, shots, sep_n, own_ref, sibling_ref, *refs):
    blocks, out_refs, sums_ref = refs[:count], refs[count : 2 * count], refs[2 * count]
    rows_ref, top_ref = refs[2 * count + 1 :]
    leaf_n = own_ref.shape[1]
    size = capacity * shots
    half = count * size
    for entry, factor_ref in enumerate((own_ref, sibling_ref)):
        for at, block in enumerate(blocks):
            for part in range(2):
                rows_ref[part * half + at * size : part * half + (at + 1) * size] = block[
                    entry * size : (entry + 1) * size, part * leaf_n : (part + 1) * leaf_n
                ]
        by_re, by_im = dot(rows_ref[...], factor_ref[0]), dot(rows_ref[...], factor_ref[1])
        solved = ((by_re[:half] - by_im[half:]).astype(BF16), (by_im[:half] + by_re[half:]).astype(BF16))
        for part in range(2):
            for at, out_ref in enumerate(out_refs):
                out_ref[entry * size : (entry + 1) * size, part * leaf_n : (part + 1) * leaf_n] = solved[part][
                    at * size : (at + 1) * size
                ]
            top_ref[entry * half : (entry + 1) * half, part * sep_n : (part + 1) * sep_n] = solved[part][:, :sep_n]
    group = lax.broadcasted_iota(jnp.int32, (sums_ref.shape[0], 2 * half), 0)
    place = lax.broadcasted_iota(jnp.int32, (sums_ref.shape[0], 2 * half), 1)
    member = one_hot(place % half // capacity == group)
    sums_ref[...] = dot(member, top_ref[...])


def tree_kernel(scales, codes_ref, sums_ref, factors_ref, out_ref):
    sep_n = factors_ref.shape[2]
    shots = out_ref.shape[0] // 2
    above = jnp.zeros(out_ref.shape, F32)
    for level in reversed(range(len(scales))):
        here = sums_ref[level * shots : (level + 1) * shots]
        path = jnp.concatenate([here[:, :sep_n], here[:, sep_n : 2 * sep_n]], axis=0)
        operand = (path * scales[level] - above).astype(BF16)
        factor = factors_ref[codes_ref[level]]
        by_re, by_im = dot(operand, factor[0]), dot(operand, factor[1])
        above = jnp.concatenate([by_re[:shots] - by_im[shots:], by_im[:shots] + by_re[shots:]], axis=0)
    out_ref[...] = above


def result_kernel(shots, capacity, place_ref, kinds_ref, above_ref, *refs):
    blocks, out_ref, back_ref = refs[:-2], refs[-2], refs[-1]
    size = blocks[0].shape[0]
    for at, block in enumerate(blocks):
        back_ref[at * size : (at + 1) * size] = block[...]
    count, width2 = out_ref.shape
    leaf_n = width2 // 2
    sep_n = above_ref.shape[1]
    _, col = slot_of(place_ref, kinds_ref, shots, capacity)
    place = lax.broadcasted_iota(jnp.int32, (count, back_ref.shape[0]), 1)
    pick = one_hot(place == col)
    shot = lax.broadcasted_iota(jnp.int32, (count, sep_n), 0) % shots
    for part in range(2):
        start = part * leaf_n
        solved = dot(pick, back_ref[:, start : start + leaf_n])
        lifted = jnp.zeros((count, sep_n), F32)
        for at in range(shots):
            here = part * shots + at
            lifted = jnp.where(shot == at, above_ref[here : here + 1], lifted)
        out_ref[:, start : start + sep_n] = (solved[:, :sep_n] - lifted).astype(BF16)
        out_ref[:, start + sep_n : start + leaf_n] = solved[:, sep_n:].astype(BF16)


def call(kernel, out_shape, args, smem=(), hbm=(), scratch=(), limit=32):
    spaces = [pltpu.SMEM if at in smem else pl.ANY if at in hbm else VMEM for at in range(len(args))]
    return pl.pallas_call(
        kernel,
        out_shape=out_shape,
        in_specs=[pl.BlockSpec(memory_space=space) for space in spaces],
        out_specs=jax.tree.map(lambda _: pl.BlockSpec(memory_space=VMEM), out_shape),
        scratch_shapes=list(scratch),
        compiler_params=pltpu.CompilerParams(vmem_limit_bytes=limit * 2**20),
    )(*args)


def on_device(sources, transmission, media, sep_code, leaf_factors, sep_factors):
    leaves, shots, width2 = sources.shape[1:]
    leaf_n = width2 // 2
    front = transmission.shape[2] // 2
    sep_lib, sep_n = sep_factors.shape[0], sep_factors.shape[2]
    nleaf = lax.axis_size("leaf")
    levels = nleaf.bit_length() - 1
    capacity = max(2, leaves * 5 // (nleaf * 2))
    pairs = nleaf // 2
    block = jax.ShapeDtypeStruct((2 * capacity * shots, width2), BF16)
    source, tau = sources[0], transmission[0][:, None, :]
    place = lax.axis_index("leaf").astype(jnp.int32).reshape(1)
    own = leaf_factors[0]
    sibling = exchange(own, 1)

    face = jax.ShapeDtypeStruct((leaves, shots, 2 * front), BF16)
    leaving = call(
        functools.partial(face_kernel, front),
        jax.ShapeDtypeStruct((leaves, shots, 2 * front), F32),
        (source, tau),
        hbm=(0, 1),
        scratch=[VMEM(face.shape, BF16)] * 2 + [VMEM(tau.shape, F32), pltpu.SemaphoreType.DMA((3,))],
    )
    arriving = from_behind(leaving, "panel")
    tau_re, tau_im = tau[..., :front], tau[..., front:]
    for _ in range(lax.axis_size("panel") - 2):
        real = arriving[..., :front] + source[..., leaf_n - front : leaf_n].astype(F32)
        imag = arriving[..., front:] + source[..., 2 * leaf_n - front :].astype(F32)
        leaving = jnp.concatenate([tau_re * real - tau_im * imag, tau_re * imag + tau_im * real], axis=-1)
        arriving = from_behind(leaving, "panel")
    arriving = after(arriving, sibling)

    kinds = jnp.repeat(media[0, :, 0], shots)[None, :]
    rows = leaves * shots
    sent = call(
        functools.partial(dispatch_kernel, shots, capacity, front),
        [block] * pairs,
        (place, kinds, source.reshape(rows, width2), arriving.reshape(rows, 2 * front)),
        smem=(0,),
        scratch=[VMEM((rows, width2), BF16)],
    )

    far = list(range(pairs // 2, pairs))
    early, late = far[: len(far) // 2], far[len(far) // 2 :]
    under_way = []

    def cross(value, at):
        if len(under_way) >= 2:
            value = after(value, under_way[-2])
        under_way.append(exchange(value, 2 * at))
        return under_way[-1]

    def solve(group, arrived):
        count = len(group)
        half = count * capacity * shots
        *solved, sums = call(
            functools.partial(leaf_kernel, count, capacity, shots, sep_n),
            [block] * count + [jax.ShapeDtypeStruct((count * shots, 2 * sep_n), F32)],
            (own, sibling, *(arrived[at] for at in group)),
            scratch=[VMEM((2 * half, leaf_n), BF16), VMEM((2 * half, 2 * sep_n), BF16)],
        )
        return dict(zip(group, solved)), sums.reshape(count, shots, 2 * sep_n)

    arrived = {0: sent[0]}
    for at in far:
        arrived[at] = cross(sent[at], at)
    near = list(range(1, pairs // 2))
    for at in near:
        arrived[at] = exchange(sent[at], 2 * at)
    solved, sums = solve([0] + near + early, arrived)
    solved_late, sums_late = solve(late, arrived)
    solved.update(solved_late)

    back = {0: solved[0]}
    for at in near:
        back[at] = exchange(solved[at], 2 * at)
    for at in far:
        back[at] = cross(solved[at], at)

    sums = jnp.concatenate([sums, sums_late], axis=0)
    code = jnp.where(jnp.arange(pairs) == 0, sep_code[0, 0], 0).astype(F32)
    share = jnp.concatenate([sums, jnp.broadcast_to(code[:, None, None], (pairs, shots, LANES))], axis=-1)
    nodes = [share]
    for _ in range(levels - 1):
        share = share.reshape((share.shape[0] // 2, 2) + share.shape[1:]).sum(axis=1)
        nodes.append(share)
    for bit in reversed(range(levels)):
        if bit:
            cut = [part.shape[0] // 2 for part in nodes]
            keep = [part[: max(1, at)] for part, at in zip(nodes, cut)]
            send = [part[at:] for part, at in zip(nodes, cut)]
        else:
            keep, send = nodes, nodes
        part = exchange(jnp.concatenate(send, axis=0), 1 << bit)
        nodes, start = [], 0
        for mine in keep:
            nodes.append(mine + part[start : start + mine.shape[0]])
            start += mine.shape[0]
    path = jnp.concatenate(nodes, axis=0)
    codes = path[:, 0, 2 * sep_n].astype(jnp.int32) % sep_lib
    scales = [1.0 / math.sqrt(leaves * 2 ** (level + 1)) for level in range(levels)]
    above = call(
        functools.partial(tree_kernel, scales),
        jax.ShapeDtypeStruct((2 * shots, sep_n), F32),
        (codes, path.reshape(levels * shots, -1), sep_factors),
        smem=(0,),
    )
    result = call(
        functools.partial(result_kernel, shots, capacity),
        jax.ShapeDtypeStruct((rows, width2), BF16),
        (place, kinds, above, *(back[at] for at in range(pairs))),
        smem=(0,),
        scratch=[VMEM((pairs * block.shape[0], width2), BF16)],
    )
    return result.reshape(1, leaves, shots, width2)


def solution(mesh):
    return jax.shard_map(
        on_device,
        mesh=mesh,
        in_specs=(
            P("panel", "leaf", None, None),
            P("panel", "leaf", None),
            P("panel", "leaf", None),
            P("panel", "leaf"),
            P("leaf", None, None, None),
            P(),
        ),
        out_specs=P("panel", "leaf", None, None),
        check_vma=False,
    )
```

```python
import functools
import math

import jax
import jax.numpy as jnp
from jax import lax
from jax.experimental import pallas as pl
from jax.experimental.pallas import tpu as pltpu
from jax.sharding import PartitionSpec as P

F32 = jnp.float32
BF16 = jnp.bfloat16
VMEM = pltpu.VMEM
LANES = 128


def from_behind(value, axis):
    count = lax.axis_size(axis)
    return lax.ppermute(value, axis, [(at, at + 1) for at in range(count - 1)])


def exchange(value, distance):
    pairs = [(at, at ^ distance) for at in range(lax.axis_size("leaf"))]
    return lax.ppermute(value, "leaf", pairs)


def dot(left, right):
    return jnp.dot(left, right, preferred_element_type=F32)


def one_hot(mask):
    return mask.astype(F32).astype(BF16)


def slot_of(place_ref, kinds_ref, shots, capacity):
    kinds = kinds_ref[...]
    count = kinds.shape[1]
    before = lax.broadcasted_iota(jnp.int32, (count, count), 0)
    later = lax.broadcasted_iota(jnp.int32, (count, count), 1)
    across = jnp.broadcast_to(kinds, (count, count))
    kinds_down = jnp.sum(jnp.where(before == later, across, 0), axis=1, keepdims=True)
    down = jnp.broadcast_to(kinds_down, (count, count))
    same = (across == down) & (before % shots == later % shots)
    rank_row = jnp.sum((same & (before < later)).astype(jnp.int32), axis=0, keepdims=True)
    rank_col = jnp.sum((same & (later < before)).astype(jnp.int32), axis=1, keepdims=True)
    shot_row = lax.broadcasted_iota(jnp.int32, (1, count), 1) % shots
    shot_col = lax.broadcasted_iota(jnp.int32, (count, 1), 0) % shots
    parity = place_ref[0] & 1
    row = ((kinds ^ parity) * shots + shot_row) * capacity + rank_row
    col = ((kinds_down ^ parity) * shots + shot_col) * capacity + rank_col
    return row, col


def face_kernel(front, source_ref, tau_ref, out_ref, re_ref, im_ref, through_ref, sems):
    leaf_n = source_ref.shape[2] // 2
    both = 2 * front
    copies = [
        pltpu.make_async_copy(source_ref.at[:, :, pl.ds(leaf_n - both, both)], re_ref, sems.at[0]),
        pltpu.make_async_copy(source_ref.at[:, :, pl.ds(2 * leaf_n - both, both)], im_ref, sems.at[1]),
        pltpu.make_async_copy(tau_ref, through_ref, sems.at[2]),
    ]
    for copy in copies:
        copy.start()
    for copy in copies:
        copy.wait()
    face_re, face_im = re_ref[...].astype(F32), im_ref[...].astype(F32)
    tau = through_ref[...]
    first = lax.broadcasted_iota(jnp.int32, tau.shape, 2) < front
    turned = pltpu.roll(tau, front, 2)
    by_same, by_other = jnp.where(first, tau, turned), jnp.where(first, -turned, tau)
    first = lax.broadcasted_iota(jnp.int32, face_re.shape, 2) < front
    face = jnp.where(first, pltpu.roll(face_re, front, 2), face_im)
    other = jnp.where(first, pltpu.roll(face_im, front, 2), face_re)
    out_ref[...] = by_same * face + by_other * other


def dispatch_kernel(shots, capacity, front, place_ref, kinds_ref, rows_ref, arriving_ref, out_ref, rhs_ref, send_ref, sems):
    leaf_n = rows_ref.shape[1] // 2
    rhs_ref[...] = rows_ref[...]
    for part in range(2):
        face = pl.ds((part + 1) * leaf_n - 2 * front, 2 * front)
        incoming = arriving_ref[...]
        lane = lax.broadcasted_iota(jnp.int32, incoming.shape, 1)
        if part == 0:
            incoming = pltpu.roll(incoming, front, 1)
        incoming = jnp.where(lane >= front, incoming, 0.0)
        rhs_ref[:, face] = (rows_ref[:, face].astype(F32) + incoming).astype(BF16)
    row, _ = slot_of(place_ref, kinds_ref, shots, capacity)
    place = lax.broadcasted_iota(jnp.int32, (send_ref.shape[0], row.shape[1]), 0)
    pick = one_hot(place == row)
    copies = []
    for part in range(2):
        columns = pl.ds(part * leaf_n, leaf_n)
        send_ref[:, columns] = dot(pick, rhs_ref[:, columns]).astype(BF16)
        copies.append(pltpu.make_async_copy(send_ref.at[:, columns], out_ref.at[:, columns], sems.at[part]))
        copies[part].start()
    for copy in copies:
        copy.wait()


def leaf_kernel(capacity, shots, sep_n, place_ref, arrived_ref, own_ref, sibling_ref, out_ref, keep_ref, send_ref, *refs):
    rows_ref, solved_ref, top_ref, sems = refs
    leaf_n = own_ref.shape[1]
    size = capacity * shots
    pairs = arrived_ref.shape[0] // (2 * size)
    half = pairs * size
    copies = []
    for entry, factor_ref in enumerate((own_ref, sibling_ref)):
        for at in range(pairs):
            first = (2 * at + entry) * size
            for part in range(2):
                rows_ref[part * half + at * size : part * half + (at + 1) * size] = arrived_ref[
                    first : first + size, part * leaf_n : (part + 1) * leaf_n
                ]
        by_re, by_im = dot(rows_ref[...], factor_ref[0]), dot(rows_ref[...], factor_ref[1])
        solved = ((by_re[:half] - by_im[half:]).astype(BF16), (by_im[:half] + by_re[half:]).astype(BF16))
        for part in range(2):
            for at in range(pairs):
                first = (2 * at + entry) * size
                solved_ref[first : first + size, part * leaf_n : (part + 1) * leaf_n] = solved[part][
                    at * size : (at + 1) * size
                ]
            top_ref[entry * half : (entry + 1) * half, part * sep_n : (part + 1) * sep_n] = solved[part][:, :sep_n]
    out = pltpu.make_async_copy(solved_ref, out_ref, sems.at[0])
    out.start()
    own_pair = place_ref[0] >> 1
    code = place_ref[1].astype(F32)
    bits = pairs.bit_length() - 1
    for other, ref in enumerate((keep_ref, send_ref)):
        count = ref.shape[0]
        row = lax.broadcasted_iota(jnp.int32, (count, 2 * half), 0)
        place = lax.broadcasted_iota(jnp.int32, (count, 2 * half), 1)
        distance = (place % half // size) ^ own_pair
        member = row < 0
        here = lax.broadcasted_iota(jnp.int32, (count, LANES), 0) < 0
        first = 0
        for level in range(bits + 1):
            nodes = max(1, 1 << bits - 1 - level) if level < bits else 1
            node = (row - first) // shots + (other * nodes if level < bits else 0)
            inside = (row >= first) & (row < first + nodes * shots)
            member |= inside & (distance >> level == node)
            if not (other and level < bits):
                lead = lax.broadcasted_iota(jnp.int32, (count, LANES), 0)
                here |= (lead >= first) & (lead < first + shots)
            first += nodes * shots
        member &= place % size // capacity == row % shots
        ref[:, : 2 * sep_n] = dot(one_hot(member), top_ref[...]).astype(ref.dtype)
        ref[:, 2 * sep_n :] = jnp.where(here, code, 0.0).astype(ref.dtype)
    out.wait()


def tree_kernel(scales, keep_ref, arrived_ref, factors_ref, out_ref):
    sep_lib, sep_n = factors_ref.shape[0], factors_ref.shape[2]
    shots = out_ref.shape[0] // 2
    sums = keep_ref[...] + arrived_ref[...].astype(F32)
    above = jnp.zeros(out_ref.shape, F32)
    for level in reversed(range(len(scales))):
        here = sums[level * shots : (level + 1) * shots]
        code = jnp.max(here[0:1, 2 * sep_n :]).astype(jnp.int32) % sep_lib
        path = jnp.concatenate([here[:, :sep_n], here[:, sep_n : 2 * sep_n]], axis=0)
        operand = (path * scales[level] - above).astype(BF16)
        factor = factors_ref[code]
        by_re, by_im = dot(operand, factor[0]), dot(operand, factor[1])
        above = jnp.concatenate([by_re[:shots] - by_im[shots:], by_im[:shots] + by_re[shots:]], axis=0)
    out_ref[...] = above


def result_kernel(shots, capacity, place_ref, kinds_ref, above_ref, back_ref, out_ref):
    count, width2 = out_ref.shape
    leaf_n = width2 // 2
    sep_n = above_ref.shape[1]
    _, col = slot_of(place_ref, kinds_ref, shots, capacity)
    place = lax.broadcasted_iota(jnp.int32, (count, back_ref.shape[0]), 1)
    pick = one_hot(place == col)
    shot = lax.broadcasted_iota(jnp.int32, (count, sep_n), 0) % shots
    for part in range(2):
        start = part * leaf_n
        solved = dot(pick, back_ref[:, start : start + leaf_n])
        lifted = jnp.zeros((count, sep_n), F32)
        for at in range(shots):
            here = part * shots + at
            lifted = jnp.where(shot == at, above_ref[here : here + 1], lifted)
        out_ref[:, start : start + sep_n] = (solved[:, :sep_n] - lifted).astype(BF16)
        out_ref[:, start + sep_n : start + leaf_n] = solved[:, sep_n:].astype(BF16)


def call(kernel, out_shape, args, smem=(), hbm=(), hbm_out=(), scratch=(), cost=None, limit=16):
    spaces = [pltpu.SMEM if at in smem else pltpu.HBM if at in hbm else VMEM for at in range(len(args))]
    shapes = out_shape if isinstance(out_shape, list) else [out_shape]
    out_specs = [pl.BlockSpec(memory_space=pltpu.HBM if at in hbm_out else VMEM) for at in range(len(shapes))]
    return pl.pallas_call(
        kernel,
        out_shape=out_shape,
        in_specs=[pl.BlockSpec(memory_space=space) for space in spaces],
        out_specs=out_specs if isinstance(out_shape, list) else out_specs[0],
        scratch_shapes=list(scratch),
        cost_estimate=cost and pl.CostEstimate(flops=cost[0], bytes_accessed=cost[1], transcendentals=0),
        compiler_params=pltpu.CompilerParams(vmem_limit_bytes=limit * 2**20),
    )(*args)


def to_pairs(value):
    groups = [list(range(parity, lax.axis_size("leaf"), 2)) for parity in range(2)]
    return lax.all_to_all(value, "leaf", 0, 0, tiled=True, axis_index_groups=groups)


def path_sums(keep, send, shots, levels):
    bits = levels - 1
    sizes = [1 << bits - 1 - level for level in range(bits)] + [1]
    arrived = exchange(send, 1 << bits)
    for bit in range(-1, bits - 1):
        sums = keep + arrived.astype(F32)
        mine, other, start = [], [], 0
        for level, count in enumerate(sizes):
            for node in range(count):
                rows = sums[start * shots : (start + 1) * shots]
                start += 1
                if level > bit or bit < 0:
                    mine.append(rows)
                    other.append(rows)
                else:
                    (other if node % 2 else mine).append(rows)
            if level <= bit:
                sizes[level] //= 2
        keep = jnp.concatenate(mine)
        arrived = exchange(jnp.concatenate(other).astype(BF16), 2 << bit if bit >= 0 else 1)
    return keep, arrived


def on_device(sources, transmission, media, sep_code, leaf_factors, sep_factors):
    leaves, shots, width2 = sources.shape[1:]
    leaf_n = width2 // 2
    front = transmission.shape[2] // 2
    sep_lib, sep_n = sep_factors.shape[0], sep_factors.shape[2]
    nleaf = lax.axis_size("leaf")
    levels = nleaf.bit_length() - 1
    capacity = max(2, leaves * 5 // (nleaf * 2))
    size = 2 * capacity * shots
    pairs = nleaf // 2
    slots = pairs * size
    source, tau = sources[0], transmission[0][:, None, :]
    place = jnp.stack([lax.axis_index("leaf").astype(jnp.int32), sep_code[0, 0] % sep_lib])
    own = leaf_factors[0]
    sibling = exchange(own, 1)

    face = jax.ShapeDtypeStruct((leaves, shots, 2 * front), BF16)
    leaving = call(
        functools.partial(face_kernel, front),
        jax.ShapeDtypeStruct((leaves, shots, 2 * front), F32),
        (source, tau),
        hbm=(0, 1),
        scratch=[VMEM(face.shape, BF16)] * 2 + [VMEM(tau.shape, F32), pltpu.SemaphoreType.DMA((3,))],
    )
    arriving = from_behind(leaving, "panel")
    tau_re, tau_im = tau[..., :front], tau[..., front:]
    for _ in range(lax.axis_size("panel") - 2):
        real = arriving[..., :front] + source[..., leaf_n - front : leaf_n].astype(F32)
        imag = arriving[..., front:] + source[..., 2 * leaf_n - front :].astype(F32)
        leaving = jnp.concatenate([tau_re * real - tau_im * imag, tau_re * imag + tau_im * real], axis=-1)
        arriving = from_behind(leaving, "panel")

    kinds = jnp.repeat(media[0, :, 0], shots)[None, :]
    rows = leaves * shots
    blocks = jax.ShapeDtypeStruct((slots, width2), BF16)
    sent = call(
        functools.partial(dispatch_kernel, shots, capacity, front),
        blocks,
        (place, kinds, source.reshape(rows, width2), arriving.reshape(rows, 2 * front)),
        smem=(0,),
        hbm_out=(0,),
        scratch=[VMEM((rows, width2), BF16), VMEM((slots, width2), BF16), pltpu.SemaphoreType.DMA((2,))],
    )
    arrived = to_pairs(sent.reshape(pairs, size, width2)).reshape(slots, width2)
    nodes = jax.ShapeDtypeStruct((pairs * shots, 2 * sep_n + LANES), F32)
    solved, keep, send = call(
        functools.partial(leaf_kernel, capacity, shots, sep_n),
        [blocks, nodes, jax.ShapeDtypeStruct(nodes.shape, BF16)],
        (place, arrived, own, sibling),
        smem=(0,),
        hbm_out=(0,),
        scratch=[
            VMEM((slots, leaf_n), BF16),
            VMEM((slots, width2), BF16),
            VMEM((slots, 2 * sep_n), BF16),
            pltpu.SemaphoreType.DMA((1,)),
        ],
    )
    back = to_pairs(solved.reshape(pairs, size, width2)).reshape(slots, width2)
    keep, arrived = path_sums(keep, send, shots, levels)
    scales = [1.0 / math.sqrt(leaves * 2 ** (level + 1)) for level in range(levels)]
    above = call(
        functools.partial(tree_kernel, scales),
        jax.ShapeDtypeStruct((2 * shots, sep_n), F32),
        (keep, arrived, sep_factors),
        cost=(1, 1),
    )
    result = call(
        functools.partial(result_kernel, shots, capacity),
        jax.ShapeDtypeStruct((rows, width2), BF16),
        (place, kinds, above, back),
        smem=(0,),
    )
    return result.reshape(1, leaves, shots, width2)


def solution(mesh):
    return jax.shard_map(
        on_device,
        mesh=mesh,
        in_specs=(
            P("panel", "leaf", None, None),
            P("panel", "leaf", None),
            P("panel", "leaf", None),
            P("panel", "leaf"),
            P("leaf", None, None, None),
            P(),
        ),
        out_specs=P("panel", "leaf", None, None),
        check_vma=False,
    )
```

```python
import functools
import math

import jax
import jax.numpy as jnp
from jax import lax
from jax.experimental import pallas as pl
from jax.experimental.pallas import tpu as pltpu
from jax.sharding import PartitionSpec as P

F32 = jnp.float32
BF16 = jnp.bfloat16
VMEM = pltpu.VMEM
LANES = 128


def from_behind(value, axis):
    count = lax.axis_size(axis)
    return lax.ppermute(value, axis, [(at, at + 1) for at in range(count - 1)])


def exchange(value, distance):
    pairs = [(at, at ^ distance) for at in range(lax.axis_size("leaf"))]
    return lax.ppermute(value, "leaf", pairs)


def dot(left, right):
    return jnp.dot(left, right, preferred_element_type=F32)


def one_hot(mask):
    return mask.astype(F32).astype(BF16)


def slot_kernel(shots, capacity, media_ref, to_slots_ref, from_slots_ref):
    slots, count = to_slots_ref.shape
    leaves = media_ref.shape[1]
    leaf = lax.broadcasted_iota(jnp.int32, (leaves, count), 0)
    of_row = one_hot(lax.broadcasted_iota(jnp.int32, (leaves, count), 1) // shots == leaf)
    kinds = dot(media_ref[...].astype(F32).astype(BF16), of_row).astype(jnp.int32)
    before = lax.broadcasted_iota(jnp.int32, (count, count), 0)
    later = lax.broadcasted_iota(jnp.int32, (count, count), 1)
    across = jnp.broadcast_to(kinds, (count, count))
    kinds_down = jnp.sum(jnp.where(before == later, across, 0), axis=1, keepdims=True)
    down = jnp.broadcast_to(kinds_down, (count, count))
    same = (across == down) & (before % shots == later % shots)
    rank_row = jnp.sum((same & (before < later)).astype(jnp.int32), axis=0, keepdims=True)
    rank_col = jnp.sum((same & (later < before)).astype(jnp.int32), axis=1, keepdims=True)
    shot_row = lax.broadcasted_iota(jnp.int32, (1, count), 1) % shots
    shot_col = lax.broadcasted_iota(jnp.int32, (count, 1), 0) % shots
    me = lax.axis_index("leaf")
    parity = me % 2
    row = ((kinds ^ me) * shots + shot_row) * capacity + rank_row
    col = ((kinds_down ^ parity) * shots + shot_col) * capacity + rank_col
    to_slots_ref[...] = one_hot(lax.broadcasted_iota(jnp.int32, (slots, count), 0) == row)
    from_slots_ref[...] = one_hot(lax.broadcasted_iota(jnp.int32, (count, slots), 1) == col)


def face_kernel(front, source_ref, tau_ref, out_ref, re_ref, im_ref, through_ref, sems):
    leaf_n = source_ref.shape[2] // 2
    both = 2 * front
    copies = [
        pltpu.make_async_copy(source_ref.at[:, :, pl.ds(leaf_n - both, both)], re_ref, sems.at[0]),
        pltpu.make_async_copy(source_ref.at[:, :, pl.ds(2 * leaf_n - both, both)], im_ref, sems.at[1]),
        pltpu.make_async_copy(tau_ref, through_ref, sems.at[2]),
    ]
    for copy in copies:
        copy.start()
    for copy in copies:
        copy.wait()
    face_re, face_im = re_ref[...].astype(F32), im_ref[...].astype(F32)
    tau = through_ref[...]
    first = lax.broadcasted_iota(jnp.int32, tau.shape, 2) < front
    turned = pltpu.roll(tau, front, 2)
    by_same, by_other = jnp.where(first, tau, turned), jnp.where(first, -turned, tau)
    first = lax.broadcasted_iota(jnp.int32, face_re.shape, 2) < front
    face = jnp.where(first, pltpu.roll(face_re, front, 2), face_im)
    other = jnp.where(first, pltpu.roll(face_im, front, 2), face_re)
    out_ref[...] = by_same * face + by_other * other


def dispatch_kernel(front, pick_ref, rows_ref, arriving_ref, _, *refs):
    out_refs, rhs_ref = refs[:-1], refs[-1]
    leaf_n = rows_ref.shape[1] // 2
    rhs_ref[...] = rows_ref[...]
    for part in range(2):
        face = pl.ds((part + 1) * leaf_n - 2 * front, 2 * front)
        incoming = arriving_ref[...]
        lane = lax.broadcasted_iota(jnp.int32, incoming.shape, 1)
        if part == 0:
            incoming = pltpu.roll(incoming, front, 1)
        incoming = jnp.where(lane >= front, incoming, 0.0)
        rhs_ref[:, face] = (rows_ref[:, face].astype(F32) + incoming).astype(BF16)
    size = out_refs[0].shape[0]
    send = dot(pick_ref[...], rhs_ref[...]).astype(BF16)
    for at, out_ref in enumerate(out_refs):
        out_ref[...] = send[at * size : (at + 1) * size]


def stage_kernel(from_ref, _, to_ref):
    to_ref[...] = from_ref[...]


def leaf_kernel(shots, sep_n, order, code_ref, own_ref, sibling_ref, *refs):
    blocks, (out_ref, keep_ref, send_ref) = dict(zip(order, refs[:-8])), refs[-8:-5]
    factor_ref, rows_ref, solved_ref, load_sems, sems = refs[-5:]
    leaf_n = own_ref.shape[1]
    loads = []
    for at in range(4):
        rows = (at // 2, pl.ds(at % 2 * (leaf_n // 2), leaf_n // 2))
        loads.append(pltpu.make_async_copy(sibling_ref.at[rows], factor_ref.at[rows], load_sems.at[at]))
        loads[at].start()
    pairs, _, size, _ = solved_ref.shape
    capacity = size // shots
    half = pairs * size
    count = keep_ref.shape[0]
    own_pair = lax.axis_index("leaf") // 2
    bits = pairs.bit_length() - 1
    row = lax.broadcasted_iota(jnp.int32, (2 * count, half), 0)
    place = lax.broadcasted_iota(jnp.int32, (2 * count, half), 1)
    lead = lax.broadcasted_iota(jnp.int32, (2 * count, LANES), 0)
    distance = place // size
    member, here, first = row < 0, lead < 0, 0
    for other in range(2):
        for level in range(bits + 1):
            nodes = 1 << bits - 1 - level if level < bits else 1
            node = (row - first) // shots + (other * nodes if level < bits else 0)
            inside = (row >= first) & (row < first + nodes * shots)
            member |= inside & (distance >> level == node)
            if not (other and level < bits):
                here |= (lead >= first) & (lead < first + shots)
            first += nodes * shots
    member = one_hot(member & (place % size // capacity == row % shots))
    codes = jnp.where(here, code_ref[0, 0].astype(F32), 0.0)

    copies, sums = [], [0.0, 0.0]
    for entry in range(2):
        for at in range(pairs):
            real = blocks[at][entry * size : (entry + 1) * size, :leaf_n]
            imag = blocks[at][entry * size : (entry + 1) * size, leaf_n:]
            first = at * size
            rows_ref[first : first + size, :leaf_n] = real
            rows_ref[first : first + size, leaf_n:] = -imag
            rows_ref[half + first : half + first + size, :leaf_n] = imag
            rows_ref[half + first : half + first + size, leaf_n:] = real
        if entry:
            for load in loads:
                load.wait()
        factor = (factor_ref if entry else own_ref)[...].reshape(2 * leaf_n, leaf_n)
        for part in range(2):
            solved = dot(rows_ref[part * half : (part + 1) * half], factor).astype(BF16)
            columns = pl.ds(part * leaf_n, leaf_n)
            for at in range(pairs):
                solved_ref[at, entry, :, columns] = solved[at * size : (at + 1) * size]
            sums[part] += dot(member, solved[:, :sep_n])
        for at in range(pairs):
            copies.append(
                pltpu.make_async_copy(
                    solved_ref.at[at, entry], out_ref.at[own_pair ^ at, entry], sems.at[entry * pairs + at]
                )
            )
            copies[-1].start()
    for ref, rows in ((keep_ref, slice(0, count)), (send_ref, slice(count, 2 * count))):
        for part in range(2):
            ref[:, part * sep_n : (part + 1) * sep_n] = sums[part][rows].astype(ref.dtype)
        ref[:, 2 * sep_n :] = codes[rows].astype(ref.dtype)
    for copy in copies:
        copy.wait()


def tree_kernel(scales, keep_ref, arrived_ref, factors_ref, out_ref):
    sep_lib, sep_n = factors_ref.shape[0], factors_ref.shape[2]
    shots = out_ref.shape[0] // 2
    sums = keep_ref[...] + arrived_ref[...].astype(F32)
    above = jnp.zeros(out_ref.shape, F32)
    for level in reversed(range(len(scales))):
        here = sums[level * shots : (level + 1) * shots]
        code = jnp.max(here[0:1, 2 * sep_n :]).astype(jnp.int32) % sep_lib
        path = jnp.concatenate([here[:, :sep_n], here[:, sep_n : 2 * sep_n]], axis=0)
        operand = (path * scales[level] - above).astype(BF16)
        factor = factors_ref[code]
        by_re, by_im = dot(operand, factor[0]), dot(operand, factor[1])
        above = jnp.concatenate([by_re[:shots] - by_im[shots:], by_im[:shots] + by_re[shots:]], axis=0)
    out_ref[...] = above


def result_kernel(shots, pick_ref, above_ref, back_ref, out_ref):
    leaves, _, width2 = out_ref.shape
    count = leaves * shots
    leaf_n = width2 // 2
    sep_n = above_ref.shape[1]
    shot = lax.broadcasted_iota(jnp.int32, (count, sep_n), 0) % shots
    for part in range(2):
        start = part * leaf_n
        solved = dot(pick_ref[...], back_ref[:, start : start + leaf_n])
        lifted = jnp.zeros((count, sep_n), F32)
        for at in range(shots):
            here = part * shots + at
            lifted = jnp.where(shot == at, above_ref[here : here + 1], lifted)
        solved = jnp.concatenate([solved[:, :sep_n] - lifted, solved[:, sep_n:]], axis=1).astype(BF16)
        out_ref[:, :, start : start + leaf_n] = solved.reshape(leaves, shots, leaf_n)


def call(kernel, out_shape, args, smem=(), hbm=(), hbm_out=(), aliases={}, scratch=(), cost=None, limit=16):
    spaces = [pltpu.SMEM if at in smem else pltpu.HBM if at in hbm else VMEM for at in range(len(args))]
    shapes = out_shape if isinstance(out_shape, list) else [out_shape]
    out_specs = [pl.BlockSpec(memory_space=pltpu.HBM if at in hbm_out else VMEM) for at in range(len(shapes))]
    return pl.pallas_call(
        kernel,
        out_shape=out_shape,
        in_specs=[pl.BlockSpec(memory_space=space) for space in spaces],
        out_specs=out_specs if isinstance(out_shape, list) else out_specs[0],
        scratch_shapes=list(scratch),
        input_output_aliases=aliases,
        cost_estimate=cost and pl.CostEstimate(flops=cost[0], bytes_accessed=cost[1], transcendentals=0),
        compiler_params=pltpu.CompilerParams(vmem_limit_bytes=limit * 2**20),
    )(*args)


def to_pairs(value):
    groups = [list(range(parity, lax.axis_size("leaf"), 2)) for parity in range(2)]
    return lax.all_to_all(value, "leaf", 0, 0, tiled=True, axis_index_groups=groups)


def path_sums(keep, send, shots, levels):
    bits = levels - 1
    sizes = [1 << bits - 1 - level for level in range(bits)] + [1]
    arrived = exchange(send, 1 << bits)
    for bit in range(-1, bits - 1):
        sums = keep + arrived.astype(F32)
        mine, other, start = [], [], 0
        for level, count in enumerate(sizes):
            for node in range(count):
                rows = sums[start * shots : (start + 1) * shots]
                start += 1
                if level > bit or bit < 0:
                    mine.append(rows)
                    other.append(rows)
                else:
                    (other if node % 2 else mine).append(rows)
            if level <= bit:
                sizes[level] //= 2
        keep = jnp.concatenate(mine)
        arrived = exchange(jnp.concatenate(other).astype(BF16), 2 << bit if bit >= 0 else 1)
    return keep, arrived


def on_device(sources, transmission, media, sep_code, leaf_factors, sep_factors):
    leaves, shots, width2 = sources.shape[1:]
    leaf_n = width2 // 2
    front = transmission.shape[2] // 2
    sep_lib, sep_n = sep_factors.shape[0], sep_factors.shape[2]
    nleaf = lax.axis_size("leaf")
    levels = nleaf.bit_length() - 1
    capacity = max(2, leaves * 5 // (nleaf * 2))
    size = 2 * capacity * shots
    pairs = nleaf // 2
    slots = pairs * size
    source, tau = sources[0], transmission[0][:, None, :]
    own = leaf_factors[0]
    sibling = exchange(own, 1)

    face = jax.ShapeDtypeStruct((leaves, shots, 2 * front), BF16)
    leaving = call(
        functools.partial(face_kernel, front),
        jax.ShapeDtypeStruct((leaves, shots, 2 * front), F32),
        (source, tau),
        hbm=(0, 1),
        scratch=[VMEM(face.shape, BF16)] * 2 + [VMEM(tau.shape, F32), pltpu.SemaphoreType.DMA((3,))],
        limit=60,
    )
    arriving = from_behind(leaving, "panel")
    tau_re, tau_im = tau[..., :front], tau[..., front:]
    for _ in range(lax.axis_size("panel") - 2):
        real = arriving[..., :front] + source[..., leaf_n - front : leaf_n].astype(F32)
        imag = arriving[..., front:] + source[..., 2 * leaf_n - front :].astype(F32)
        leaving = jnp.concatenate([tau_re * real - tau_im * imag, tau_re * imag + tau_im * real], axis=-1)
        arriving = from_behind(leaving, "panel")

    rows = leaves * shots
    to_slots, from_slots = call(
        functools.partial(slot_kernel, shots, capacity),
        [jax.ShapeDtypeStruct((slots, rows), BF16), jax.ShapeDtypeStruct((rows, slots), BF16)],
        (media[0].reshape(1, leaves),),
    )
    block = jax.ShapeDtypeStruct((size, width2), BF16)
    sent = call(
        functools.partial(dispatch_kernel, front),
        [block] * pairs,
        (to_slots, source.reshape(rows, width2), arriving.reshape(rows, 2 * front), sibling),
        hbm=(3,),
        scratch=[VMEM((rows, width2), BF16)],
    )
    far, near = list(range(pairs // 2, pairs)), list(range(1, pairs // 2))
    order = far[-1:] + near + far[-2::-1] + [0]
    arrived = {at: exchange(sent[at], 2 * at) if at else sent[at] for at in order}
    own = call(stage_kernel, jax.ShapeDtypeStruct(own.shape, BF16), (own, sent[0]), hbm=(1,))
    nodes = jax.ShapeDtypeStruct((pairs * shots, 2 * sep_n + LANES), F32)
    halves = (pairs, 2, size // 2, width2)
    solved, keep, send = call(
        functools.partial(leaf_kernel, shots, sep_n, order),
        [jax.ShapeDtypeStruct(halves, BF16), nodes, jax.ShapeDtypeStruct(nodes.shape, BF16)],
        (sep_code % sep_lib, own, sibling, *(arrived[at] for at in order)),
        smem=(0,),
        hbm=(2,),
        hbm_out=(0,),
        scratch=[
            VMEM(own.shape, BF16),
            VMEM((slots, width2), BF16),
            VMEM(halves, BF16),
            pltpu.SemaphoreType.DMA((4,)),
            pltpu.SemaphoreType.DMA((2 * pairs,)),
        ],
    )
    back = to_pairs(solved.reshape(pairs, size, width2)).reshape(slots, width2)
    keep, arrived = path_sums(keep, send, shots, levels)
    scales = [1.0 / math.sqrt(leaves * 2 ** (level + 1)) for level in range(levels)]
    above = call(
        functools.partial(tree_kernel, scales),
        jax.ShapeDtypeStruct((2 * shots, sep_n), F32),
        (keep, arrived, sep_factors),
        cost=(1, 1),
    )
    result = call(
        functools.partial(result_kernel, shots),
        jax.ShapeDtypeStruct((leaves, shots, width2), BF16),
        (from_slots, above, back),
    )
    return result[None]


def solution(mesh):
    return jax.shard_map(
        on_device,
        mesh=mesh,
        in_specs=(
            P("panel", "leaf", None, None),
            P("panel", "leaf", None),
            P("panel", "leaf", None),
            P("panel", "leaf"),
            P("leaf", None, None, None),
            P(),
        ),
        out_specs=P("panel", "leaf", None, None),
        check_vma=False,
    )
```

```python
import functools
import math

import jax
import jax.numpy as jnp
from jax import lax
from jax.experimental import pallas as pl
from jax.experimental.pallas import tpu as pltpu
from jax.sharding import PartitionSpec as P

F32 = jnp.float32
BF16 = jnp.bfloat16
VMEM = pltpu.VMEM
LANES = 128


def from_behind(value, axis):
    count = lax.axis_size(axis)
    return lax.ppermute(value, axis, [(at, at + 1) for at in range(count - 1)])


def exchange(value, distance):
    pairs = [(at, at ^ distance) for at in range(lax.axis_size("leaf"))]
    return lax.ppermute(value, "leaf", pairs)


def dot(left, right):
    return jnp.dot(left, right, preferred_element_type=F32)


def one_hot(mask):
    return mask.astype(F32).astype(BF16)


def slot_kernel(shots, capacity, media_ref, to_slots_ref, from_slots_ref):
    slots, count = to_slots_ref.shape
    leaves = media_ref.shape[1]
    leaf = lax.broadcasted_iota(jnp.int32, (leaves, count), 0)
    of_row = one_hot(lax.broadcasted_iota(jnp.int32, (leaves, count), 1) // shots == leaf)
    kinds = dot(media_ref[...].astype(F32).astype(BF16), of_row).astype(jnp.int32)
    before = lax.broadcasted_iota(jnp.int32, (count, count), 0)
    later = lax.broadcasted_iota(jnp.int32, (count, count), 1)
    across = jnp.broadcast_to(kinds, (count, count))
    kinds_down = jnp.sum(jnp.where(before == later, across, 0), axis=1, keepdims=True)
    down = jnp.broadcast_to(kinds_down, (count, count))
    same = (across == down) & (before % shots == later % shots)
    rank_row = jnp.sum((same & (before < later)).astype(jnp.int32), axis=0, keepdims=True)
    rank_col = jnp.sum((same & (later < before)).astype(jnp.int32), axis=1, keepdims=True)
    shot_row = lax.broadcasted_iota(jnp.int32, (1, count), 1) % shots
    shot_col = lax.broadcasted_iota(jnp.int32, (count, 1), 0) % shots
    me = lax.axis_index("leaf")
    parity = me % 2
    row = ((kinds ^ me) * shots + shot_row) * capacity + rank_row
    col = ((kinds_down ^ parity) * shots + shot_col) * capacity + rank_col
    to_slots_ref[...] = one_hot(lax.broadcasted_iota(jnp.int32, (slots, count), 0) == row)
    from_slots_ref[...] = one_hot(lax.broadcasted_iota(jnp.int32, (count, slots), 1) == col)


def face_kernel(front, source_ref, tau_ref, out_ref, re_ref, im_ref, through_ref, sems):
    leaf_n = source_ref.shape[2] // 2
    both = 2 * front
    copies = [
        pltpu.make_async_copy(source_ref.at[:, :, pl.ds(leaf_n - both, both)], re_ref, sems.at[0]),
        pltpu.make_async_copy(source_ref.at[:, :, pl.ds(2 * leaf_n - both, both)], im_ref, sems.at[1]),
        pltpu.make_async_copy(tau_ref, through_ref, sems.at[2]),
    ]
    for copy in copies:
        copy.start()
    for copy in copies:
        copy.wait()
    face_re, face_im = re_ref[...].astype(F32), im_ref[...].astype(F32)
    tau = through_ref[...]
    first = lax.broadcasted_iota(jnp.int32, tau.shape, 2) < front
    turned = pltpu.roll(tau, front, 2)
    by_same, by_other = jnp.where(first, tau, turned), jnp.where(first, -turned, tau)
    first = lax.broadcasted_iota(jnp.int32, face_re.shape, 2) < front
    face = jnp.where(first, pltpu.roll(face_re, front, 2), face_im)
    other = jnp.where(first, pltpu.roll(face_im, front, 2), face_re)
    out_ref[...] = by_same * face + by_other * other


def dispatch_kernel(front, pick_ref, rows_ref, arriving_ref, _, *refs):
    out_refs, rhs_ref = refs[:-1], refs[-1]
    leaf_n = rows_ref.shape[1] // 2
    rhs_ref[...] = rows_ref[...]
    for part in range(2):
        face = pl.ds((part + 1) * leaf_n - 2 * front, 2 * front)
        incoming = arriving_ref[...]
        lane = lax.broadcasted_iota(jnp.int32, incoming.shape, 1)
        if part == 0:
            incoming = pltpu.roll(incoming, front, 1)
        incoming = jnp.where(lane >= front, incoming, 0.0)
        rhs_ref[:, face] = (rows_ref[:, face].astype(F32) + incoming).astype(BF16)
    size = out_refs[0].shape[0]
    send = dot(pick_ref[...], rhs_ref[...]).astype(BF16)
    for at, out_ref in enumerate(out_refs):
        out_ref[...] = send[at * size : (at + 1) * size]


def stage_kernel(own_ref, sibling_ref, _, *to_refs):
    to_refs[0][...] = own_ref[...]
    to_refs[1][...] = sibling_ref[...]


def leaf_kernel(shots, sep_n, group, pairs, own_ref, sibling_ref, *refs):
    blocks, refs = refs[: len(group)], refs[len(group) :]
    if len(refs) == 5:
        code_ref = None
        out_ref, sums_ref, rows_ref, solved_ref, sems = refs
        count = sums_ref.shape[0]
    else:
        code_ref, before_ref, _, out_ref, keep_ref, send_ref, rows_ref, solved_ref, sems = refs
        count = 2 * keep_ref.shape[0]
    leaf_n = own_ref.shape[1]
    members, _, size, _ = solved_ref.shape
    capacity = size // shots
    half = members * size
    own_pair = lax.axis_index("leaf") // 2
    bits = pairs.bit_length() - 1
    row = lax.broadcasted_iota(jnp.int32, (count, half), 0)
    place = lax.broadcasted_iota(jnp.int32, (count, half), 1)
    lead = lax.broadcasted_iota(jnp.int32, (count, LANES), 0)
    distance = jnp.zeros((count, half), jnp.int32)
    for at, block in enumerate(group):
        distance = jnp.where(place // size == at, block, distance)
    member, here, first = row < 0, lead < 0, 0
    for other in range(2):
        for level in range(bits + 1):
            nodes = 1 << bits - 1 - level if level < bits else 1
            node = (row - first) // shots + (other * nodes if level < bits else 0)
            inside = (row >= first) & (row < first + nodes * shots)
            member |= inside & (distance >> level == node)
            if not (other and level < bits):
                here |= (lead >= first) & (lead < first + shots)
            first += nodes * shots
    member = one_hot(member & (place % size // capacity == row % shots))

    copies, sums = [], [0.0, 0.0]
    for entry in range(2):
        for at in range(members):
            real = blocks[at][entry * size : (entry + 1) * size, :leaf_n]
            imag = blocks[at][entry * size : (entry + 1) * size, leaf_n:]
            first = at * size
            rows_ref[first : first + size, :leaf_n] = real
            rows_ref[first : first + size, leaf_n:] = -imag
            rows_ref[half + first : half + first + size, :leaf_n] = imag
            rows_ref[half + first : half + first + size, leaf_n:] = real
        factor = (sibling_ref if entry else own_ref)[...].reshape(2 * leaf_n, leaf_n)
        both = dot(rows_ref[...], factor).astype(BF16)
        for part in range(2):
            solved = both[part * half : (part + 1) * half]
            columns = pl.ds(part * leaf_n, leaf_n)
            for at in range(members):
                solved_ref[at, entry, :, columns] = solved[at * size : (at + 1) * size]
            sums[part] += dot(member, solved[:, :sep_n])
        for at, block in enumerate(group):
            copies.append(
                pltpu.make_async_copy(
                    solved_ref.at[at, entry], out_ref.at[own_pair ^ block, entry], sems.at[entry * members + at]
                )
            )
            copies[-1].start()
    for part in range(2):
        columns = slice(part * sep_n, (part + 1) * sep_n)
        if code_ref is None:
            sums_ref[:, columns] = sums[part]
        else:
            total = sums[part] + before_ref[:, columns]
            keep_ref[:, columns] = total[: count // 2]
            send_ref[:, columns] = total[count // 2 :].astype(BF16)
    if code_ref is not None:
        codes = jnp.where(here, code_ref[0, 0].astype(F32), 0.0)
        keep_ref[:, 2 * sep_n :] = codes[: count // 2]
        send_ref[:, 2 * sep_n :] = codes[count // 2 :].astype(BF16)
    for copy in copies:
        copy.wait()


def tree_kernel(scales, keep_ref, arrived_ref, factors_ref, out_ref):
    sep_lib, sep_n = factors_ref.shape[0], factors_ref.shape[2]
    shots = out_ref.shape[0] // 2
    sums = keep_ref[...] + arrived_ref[...].astype(F32)
    above = jnp.zeros(out_ref.shape, F32)
    for level in reversed(range(len(scales))):
        here = sums[level * shots : (level + 1) * shots]
        code = jnp.max(here[0:1, 2 * sep_n :]).astype(jnp.int32) % sep_lib
        path = jnp.concatenate([here[:, :sep_n], here[:, sep_n : 2 * sep_n]], axis=0)
        operand = (path * scales[level] - above).astype(BF16)
        factor = factors_ref[code]
        by_re, by_im = dot(operand, factor[0]), dot(operand, factor[1])
        above = jnp.concatenate([by_re[:shots] - by_im[shots:], by_im[:shots] + by_re[shots:]], axis=0)
    out_ref[...] = above


def result_kernel(shots, pick_ref, above_ref, back_ref, out_ref):
    leaves, _, width2 = out_ref.shape
    count = leaves * shots
    leaf_n = width2 // 2
    sep_n = above_ref.shape[1]
    shot = lax.broadcasted_iota(jnp.int32, (count, sep_n), 0) % shots
    for part in range(2):
        start = part * leaf_n
        solved = dot(pick_ref[...], back_ref[:, start : start + leaf_n])
        lifted = jnp.zeros((count, sep_n), F32)
        for at in range(shots):
            here = part * shots + at
            lifted = jnp.where(shot == at, above_ref[here : here + 1], lifted)
        solved = jnp.concatenate([solved[:, :sep_n] - lifted, solved[:, sep_n:]], axis=1).astype(BF16)
        out_ref[:, :, start : start + leaf_n] = solved.reshape(leaves, shots, leaf_n)


def call(kernel, out_shape, args, smem=(), hbm=(), hbm_out=(), aliases={}, scratch=(), cost=None, limit=16):
    spaces = [pltpu.SMEM if at in smem else pltpu.HBM if at in hbm else VMEM for at in range(len(args))]
    shapes = out_shape if isinstance(out_shape, list) else [out_shape]
    out_specs = [pl.BlockSpec(memory_space=pltpu.HBM if at in hbm_out else VMEM) for at in range(len(shapes))]
    return pl.pallas_call(
        kernel,
        out_shape=out_shape,
        in_specs=[pl.BlockSpec(memory_space=space) for space in spaces],
        out_specs=out_specs if isinstance(out_shape, list) else out_specs[0],
        scratch_shapes=list(scratch),
        input_output_aliases=aliases,
        cost_estimate=cost and pl.CostEstimate(flops=cost[0], bytes_accessed=cost[1], transcendentals=0),
        compiler_params=pltpu.CompilerParams(vmem_limit_bytes=limit * 2**20),
    )(*args)


def to_pairs(value):
    groups = [list(range(parity, lax.axis_size("leaf"), 2)) for parity in range(2)]
    return lax.all_to_all(value, "leaf", 0, 0, tiled=True, axis_index_groups=groups)


def path_sums(keep, send, shots, levels):
    bits = levels - 1
    sizes = [1 << bits - 1 - level for level in range(bits)] + [1]
    arrived = exchange(send, 1 << bits)
    for bit in range(-1, bits - 1):
        sums = keep + arrived.astype(F32)
        mine, other, start = [], [], 0
        for level, count in enumerate(sizes):
            for node in range(count):
                rows = sums[start * shots : (start + 1) * shots]
                start += 1
                if level > bit or bit < 0:
                    mine.append(rows)
                    other.append(rows)
                else:
                    (other if node % 2 else mine).append(rows)
            if level <= bit:
                sizes[level] //= 2
        keep = jnp.concatenate(mine)
        arrived = exchange(jnp.concatenate(other).astype(BF16), 2 << bit if bit >= 0 else 1)
    return keep, arrived


def on_device(sources, transmission, media, sep_code, leaf_factors, sep_factors):
    leaves, shots, width2 = sources.shape[1:]
    leaf_n = width2 // 2
    front = transmission.shape[2] // 2
    sep_lib, sep_n = sep_factors.shape[0], sep_factors.shape[2]
    nleaf = lax.axis_size("leaf")
    levels = nleaf.bit_length() - 1
    capacity = max(2, leaves * 5 // (nleaf * 2))
    size = 2 * capacity * shots
    pairs = nleaf // 2
    slots = pairs * size
    source, tau = sources[0], transmission[0][:, None, :]
    own = leaf_factors[0]
    sibling = exchange(own, 1)

    face = jax.ShapeDtypeStruct((leaves, shots, 2 * front), BF16)
    leaving = call(
        functools.partial(face_kernel, front),
        jax.ShapeDtypeStruct((leaves, shots, 2 * front), F32),
        (source, tau),
        hbm=(0, 1),
        scratch=[VMEM(face.shape, BF16)] * 2 + [VMEM(tau.shape, F32), pltpu.SemaphoreType.DMA((3,))],
        limit=60,
    )
    arriving = from_behind(leaving, "panel")
    tau_re, tau_im = tau[..., :front], tau[..., front:]
    for _ in range(lax.axis_size("panel") - 2):
        real = arriving[..., :front] + source[..., leaf_n - front : leaf_n].astype(F32)
        imag = arriving[..., front:] + source[..., 2 * leaf_n - front :].astype(F32)
        leaving = jnp.concatenate([tau_re * real - tau_im * imag, tau_re * imag + tau_im * real], axis=-1)
        arriving = from_behind(leaving, "panel")

    rows = leaves * shots
    to_slots, from_slots = call(
        functools.partial(slot_kernel, shots, capacity),
        [jax.ShapeDtypeStruct((slots, rows), BF16), jax.ShapeDtypeStruct((rows, slots), BF16)],
        (media[0].reshape(1, leaves),),
    )
    block = jax.ShapeDtypeStruct((size, width2), BF16)
    sent = call(
        functools.partial(dispatch_kernel, front),
        [block] * pairs,
        (to_slots, source.reshape(rows, width2), arriving.reshape(rows, 2 * front), sibling),
        hbm=(3,),
        scratch=[VMEM((rows, width2), BF16)],
    )
    far, near = list(range(pairs // 2, pairs)), list(range(1, pairs // 2))
    order = far[-1:] + near + far[-2::-1] + [0]
    arrived = {at: exchange(sent[at], 2 * at) if at else sent[at] for at in order}
    own, sibling = call(stage_kernel, [jax.ShapeDtypeStruct(own.shape, BF16)] * 2, (own, sibling, sent[0]), hbm=(2,))
    nodes = jax.ShapeDtypeStruct((pairs * shots, 2 * sep_n + LANES), F32)
    halves = (pairs, 2, size // 2, width2)
    first, last = order[: pairs // 2] + [0], order[pairs // 2 : -1]

    def scratch(group):
        return [
            VMEM((len(group) * size, width2), BF16),
            VMEM((len(group),) + halves[1:], BF16),
            pltpu.SemaphoreType.DMA((2 * len(group),)),
        ]

    solved, sums = call(
        functools.partial(leaf_kernel, shots, sep_n, first, pairs),
        [jax.ShapeDtypeStruct(halves, BF16), jax.ShapeDtypeStruct((2 * pairs * shots, 2 * sep_n), F32)],
        (own, sibling, *(arrived[at] for at in first)),
        hbm_out=(0,),
        scratch=scratch(first),
    )
    solved, keep, send = call(
        functools.partial(leaf_kernel, shots, sep_n, last, pairs),
        [jax.ShapeDtypeStruct(halves, BF16), nodes, jax.ShapeDtypeStruct(nodes.shape, BF16)],
        (own, sibling, *(arrived[at] for at in last), sep_code % sep_lib, sums, solved),
        smem=(2 + len(last),),
        hbm=(4 + len(last),),
        hbm_out=(0,),
        aliases={4 + len(last): 0},
        scratch=scratch(last),
    )
    back = to_pairs(solved.reshape(pairs, size, width2)).reshape(slots, width2)
    keep, arrived = path_sums(keep, send, shots, levels)
    scales = [1.0 / math.sqrt(leaves * 2 ** (level + 1)) for level in range(levels)]
    above = call(
        functools.partial(tree_kernel, scales),
        jax.ShapeDtypeStruct((2 * shots, sep_n), F32),
        (keep, arrived, sep_factors),
        cost=(1, 1),
    )
    result = call(
        functools.partial(result_kernel, shots),
        jax.ShapeDtypeStruct((leaves, shots, width2), BF16),
        (from_slots, above, back),
    )
    return result[None]


def solution(mesh):
    return jax.shard_map(
        on_device,
        mesh=mesh,
        in_specs=(
            P("panel", "leaf", None, None),
            P("panel", "leaf", None),
            P("panel", "leaf", None),
            P("panel", "leaf"),
            P("leaf", None, None, None),
            P(),
        ),
        out_specs=P("panel", "leaf", None, None),
        check_vma=False,
    )
```

```python
import functools
import math

import jax
import jax.numpy as jnp
from jax import lax
from jax.experimental import pallas as pl
from jax.experimental.pallas import tpu as pltpu
from jax.sharding import PartitionSpec as P

F32 = jnp.float32
BF16 = jnp.bfloat16
VMEM = pltpu.VMEM
LANES = 128


def around(value, axis):
    count = lax.axis_size(axis)
    return lax.ppermute(value, axis, [(at, (at + 1) % count) for at in range(count)])


def exchange(value, distance):
    pairs = [(at, at ^ distance) for at in range(lax.axis_size("leaf"))]
    return lax.ppermute(value, "leaf", pairs)


def dot(left, right):
    return jnp.dot(left, right, preferred_element_type=F32)


def one_hot(mask):
    return mask.astype(F32).astype(BF16)


def slot_kernel(shots, capacity, media_ref, to_slots_ref, from_slots_ref):
    slots, count = to_slots_ref.shape
    leaves = media_ref.shape[1]
    leaf = lax.broadcasted_iota(jnp.int32, (leaves, count), 0)
    of_row = one_hot(lax.broadcasted_iota(jnp.int32, (leaves, count), 1) // shots == leaf)
    kinds = dot(media_ref[...].astype(F32).astype(BF16), of_row).astype(jnp.int32)
    before = lax.broadcasted_iota(jnp.int32, (count, count), 0)
    later = lax.broadcasted_iota(jnp.int32, (count, count), 1)
    across = jnp.broadcast_to(kinds, (count, count))
    kinds_down = jnp.sum(jnp.where(before == later, across, 0), axis=1, keepdims=True)
    down = jnp.broadcast_to(kinds_down, (count, count))
    same = (across == down) & (before % shots == later % shots)
    rank_row = jnp.sum((same & (before < later)).astype(jnp.int32), axis=0, keepdims=True)
    rank_col = jnp.sum((same & (later < before)).astype(jnp.int32), axis=1, keepdims=True)
    shot_row = lax.broadcasted_iota(jnp.int32, (1, count), 1) % shots
    shot_col = lax.broadcasted_iota(jnp.int32, (count, 1), 0) % shots
    me = lax.axis_index("leaf")
    parity = me % 2
    row = ((kinds ^ me) * shots + shot_row) * capacity + rank_row
    col = ((kinds_down ^ parity) * shots + shot_col) * capacity + rank_col
    to_slots_ref[...] = one_hot(lax.broadcasted_iota(jnp.int32, (slots, count), 0) == row)
    from_slots_ref[...] = one_hot(lax.broadcasted_iota(jnp.int32, (count, slots), 1) == col)


def face_kernel(front, source_ref, tau_ref, out_ref, re_ref, im_ref, through_ref, sems):
    leaf_n = source_ref.shape[2] // 2
    both = 2 * front
    copies = [
        pltpu.make_async_copy(source_ref.at[:, :, pl.ds(leaf_n - both, both)], re_ref, sems.at[0]),
        pltpu.make_async_copy(source_ref.at[:, :, pl.ds(2 * leaf_n - both, both)], im_ref, sems.at[1]),
        pltpu.make_async_copy(tau_ref, through_ref, sems.at[2]),
    ]
    for copy in copies:
        copy.start()
    for copy in copies:
        copy.wait()
    face_re, face_im = re_ref[...].astype(F32), im_ref[...].astype(F32)
    tau = through_ref[...]
    first = lax.broadcasted_iota(jnp.int32, tau.shape, 2) < front
    turned = pltpu.roll(tau, front, 2)
    by_same, by_other = jnp.where(first, tau, turned), jnp.where(first, -turned, tau)
    first = lax.broadcasted_iota(jnp.int32, face_re.shape, 2) < front
    face = jnp.where(first, pltpu.roll(face_re, front, 2), face_im)
    other = jnp.where(first, pltpu.roll(face_im, front, 2), face_re)
    out_ref[...] = (by_same * face + by_other * other).reshape(out_ref.shape).astype(BF16)


def dispatch_kernel(front, pick_ref, rows_ref, arriving_ref, _, *refs):
    out_refs, rhs_ref = refs[:-1], refs[-1]
    leaf_n = rows_ref.shape[1] // 2
    rhs_ref[...] = rows_ref[...]
    for part in range(2):
        face = pl.ds((part + 1) * leaf_n - 2 * front, 2 * front)
        incoming = arriving_ref[...].astype(F32)
        lane = lax.broadcasted_iota(jnp.int32, incoming.shape, 1)
        if part == 0:
            incoming = pltpu.roll(incoming, front, 1)
        incoming = jnp.where((lane >= front) & (lax.axis_index("panel") > 0), incoming, 0.0)
        rhs_ref[:, face] = (rows_ref[:, face].astype(F32) + incoming).astype(BF16)
    size = out_refs[0].shape[0]
    send = dot(pick_ref[...], rhs_ref[...]).astype(BF16)
    for at, out_ref in enumerate(out_refs):
        out_ref[...] = send[at * size : (at + 1) * size]


def stage_kernel(own_ref, sibling_ref, _, *to_refs):
    to_refs[0][...] = own_ref[...]
    to_refs[1][...] = sibling_ref[...]


def leaf_kernel(shots, sep_n, group, pairs, own_ref, sibling_ref, *refs):
    blocks, refs = refs[: len(group)], refs[len(group) :]
    if len(refs) == 5:
        code_ref = None
        out_ref, sums_ref, rows_ref, solved_ref, sems = refs
        count = sums_ref.shape[0]
    else:
        code_ref, before_ref, _, out_ref, keep_ref, send_ref, rows_ref, solved_ref, sems = refs
        count = 2 * keep_ref.shape[0]
    leaf_n = own_ref.shape[1]
    members, _, size, _ = solved_ref.shape
    capacity = size // shots
    half = members * size
    own_pair = lax.axis_index("leaf") // 2
    bits = pairs.bit_length() - 1
    row = lax.broadcasted_iota(jnp.int32, (count, half), 0)
    place = lax.broadcasted_iota(jnp.int32, (count, half), 1)
    lead = lax.broadcasted_iota(jnp.int32, (count, LANES), 0)
    distance = jnp.zeros((count, half), jnp.int32)
    for at, block in enumerate(group):
        distance = jnp.where(place // size == at, block, distance)
    member, here, first = row < 0, lead < 0, 0
    for other in range(2):
        for level in range(bits + 1):
            nodes = 1 << bits - 1 - level if level < bits else 1
            node = (row - first) // shots + (other * nodes if level < bits else 0)
            inside = (row >= first) & (row < first + nodes * shots)
            member |= inside & (distance >> level == node)
            if not (other and level < bits):
                here |= (lead >= first) & (lead < first + shots)
            first += nodes * shots
    member = one_hot(member & (place % size // capacity == row % shots))

    copies, sums = [], [0.0, 0.0]
    for entry in range(2):
        for at in range(members):
            real = blocks[at][entry * size : (entry + 1) * size, :leaf_n]
            imag = blocks[at][entry * size : (entry + 1) * size, leaf_n:]
            first = at * size
            rows_ref[first : first + size, :leaf_n] = real
            rows_ref[first : first + size, leaf_n:] = -imag
            rows_ref[half + first : half + first + size, :leaf_n] = imag
            rows_ref[half + first : half + first + size, leaf_n:] = real
        factor = (sibling_ref if entry else own_ref)[...].reshape(2 * leaf_n, leaf_n)
        both = dot(rows_ref[...], factor).astype(BF16)
        for part in range(2):
            solved = both[part * half : (part + 1) * half]
            columns = pl.ds(part * leaf_n, leaf_n)
            for at in range(members):
                solved_ref[at, entry, :, columns] = solved[at * size : (at + 1) * size]
            sums[part] += dot(member, solved[:, :sep_n])
        for at, block in enumerate(group):
            copies.append(
                pltpu.make_async_copy(
                    solved_ref.at[at, entry], out_ref.at[own_pair ^ block, entry], sems.at[entry * members + at]
                )
            )
            copies[-1].start()
    for part in range(2):
        columns = slice(part * sep_n, (part + 1) * sep_n)
        if code_ref is None:
            sums_ref[:, columns] = sums[part]
        else:
            total = sums[part] + before_ref[:, columns]
            keep_ref[:, columns] = total[: count // 2]
            send_ref[:, columns] = total[count // 2 :].astype(BF16)
    if code_ref is not None:
        codes = jnp.where(here, code_ref[0, 0].astype(F32), 0.0)
        keep_ref[:, 2 * sep_n :] = codes[: count // 2]
        send_ref[:, 2 * sep_n :] = codes[count // 2 :].astype(BF16)
    for copy in copies:
        copy.wait()


def tree_kernel(scales, keep_ref, arrived_ref, factors_ref, out_ref):
    sep_lib, sep_n = factors_ref.shape[0], factors_ref.shape[2]
    shots = out_ref.shape[0] // 2
    sums = keep_ref[...] + arrived_ref[...].astype(F32)
    above = jnp.zeros(out_ref.shape, F32)
    for level in reversed(range(len(scales))):
        here = sums[level * shots : (level + 1) * shots]
        code = jnp.max(here[0:1, 2 * sep_n :]).astype(jnp.int32) % sep_lib
        path = jnp.concatenate([here[:, :sep_n], here[:, sep_n : 2 * sep_n]], axis=0)
        operand = (path * scales[level] - above).astype(BF16)
        factor = factors_ref[code]
        by_re, by_im = dot(operand, factor[0]), dot(operand, factor[1])
        above = jnp.concatenate([by_re[:shots] - by_im[shots:], by_im[:shots] + by_re[shots:]], axis=0)
    out_ref[...] = above


def result_kernel(shots, pick_ref, above_ref, back_ref, out_ref):
    leaves, _, width2 = out_ref.shape
    count = leaves * shots
    leaf_n = width2 // 2
    sep_n = above_ref.shape[1]
    shot = lax.broadcasted_iota(jnp.int32, (count, sep_n), 0) % shots
    for part in range(2):
        start = part * leaf_n
        solved = dot(pick_ref[...], back_ref[:, start : start + leaf_n])
        lifted = jnp.zeros((count, sep_n), F32)
        for at in range(shots):
            here = part * shots + at
            lifted = jnp.where(shot == at, above_ref[here : here + 1], lifted)
        solved = jnp.concatenate([solved[:, :sep_n] - lifted, solved[:, sep_n:]], axis=1).astype(BF16)
        out_ref[:, :, start : start + leaf_n] = solved.reshape(leaves, shots, leaf_n)


def call(kernel, out_shape, args, smem=(), hbm=(), hbm_out=(), aliases={}, scratch=(), cost=None, limit=16):
    spaces = [pltpu.SMEM if at in smem else pltpu.HBM if at in hbm else VMEM for at in range(len(args))]
    shapes = out_shape if isinstance(out_shape, list) else [out_shape]
    out_specs = [pl.BlockSpec(memory_space=pltpu.HBM if at in hbm_out else VMEM) for at in range(len(shapes))]
    return pl.pallas_call(
        kernel,
        out_shape=out_shape,
        in_specs=[pl.BlockSpec(memory_space=space) for space in spaces],
        out_specs=out_specs if isinstance(out_shape, list) else out_specs[0],
        scratch_shapes=list(scratch),
        input_output_aliases=aliases,
        cost_estimate=cost and pl.CostEstimate(flops=cost[0], bytes_accessed=cost[1], transcendentals=0),
        compiler_params=pltpu.CompilerParams(vmem_limit_bytes=limit * 2**20),
    )(*args)


def to_pairs(value):
    groups = [list(range(parity, lax.axis_size("leaf"), 2)) for parity in range(2)]
    return lax.all_to_all(value, "leaf", 0, 0, tiled=True, axis_index_groups=groups)


def path_sums(keep, send, shots, levels):
    bits = levels - 1
    sizes = [1 << bits - 1 - level for level in range(bits)] + [1]
    arrived = exchange(send, 1 << bits)
    for bit in range(-1, bits - 1):
        sums = keep + arrived.astype(F32)
        mine, other, start = [], [], 0
        for level, count in enumerate(sizes):
            for node in range(count):
                rows = sums[start * shots : (start + 1) * shots]
                start += 1
                if level > bit or bit < 0:
                    mine.append(rows)
                    other.append(rows)
                else:
                    (other if node % 2 else mine).append(rows)
            if level <= bit:
                sizes[level] //= 2
        keep = jnp.concatenate(mine)
        arrived = exchange(jnp.concatenate(other).astype(BF16), 2 << bit if bit >= 0 else 1)
    return keep, arrived


def on_device(sources, transmission, media, sep_code, leaf_factors, sep_factors):
    leaves, shots, width2 = sources.shape[1:]
    leaf_n = width2 // 2
    front = transmission.shape[2] // 2
    sep_lib, sep_n = sep_factors.shape[0], sep_factors.shape[2]
    nleaf = lax.axis_size("leaf")
    levels = nleaf.bit_length() - 1
    capacity = max(2, leaves * 5 // (nleaf * 2))
    size = 2 * capacity * shots
    pairs = nleaf // 2
    slots = pairs * size
    source, tau = sources[0], transmission[0][:, None, :]
    own = leaf_factors[0]
    sibling = exchange(own, 1)

    face = jax.ShapeDtypeStruct((leaves, shots, 2 * front), BF16)
    rows = leaves * shots
    leaving = call(
        functools.partial(face_kernel, front),
        jax.ShapeDtypeStruct((rows, 2 * front), BF16),
        (source, tau),
        hbm=(0, 1),
        scratch=[VMEM(face.shape, BF16)] * 2 + [VMEM(tau.shape, F32), pltpu.SemaphoreType.DMA((3,))],
        limit=60,
    )
    arriving = around(leaving, "panel")
    tau_re, tau_im = tau[..., :front], tau[..., front:]
    for _ in range(lax.axis_size("panel") - 2):
        arriving = jnp.where(lax.axis_index("panel") > 0, arriving, 0).reshape(face.shape).astype(F32)
        real = arriving[..., :front] + source[..., leaf_n - front : leaf_n].astype(F32)
        imag = arriving[..., front:] + source[..., 2 * leaf_n - front :].astype(F32)
        leaving = jnp.concatenate([tau_re * real - tau_im * imag, tau_re * imag + tau_im * real], axis=-1)
        arriving = around(leaving.reshape(rows, 2 * front).astype(BF16), "panel")

    to_slots, from_slots = call(
        functools.partial(slot_kernel, shots, capacity),
        [jax.ShapeDtypeStruct((slots, rows), BF16), jax.ShapeDtypeStruct((rows, slots), BF16)],
        (media[0].reshape(1, leaves),),
    )
    block = jax.ShapeDtypeStruct((size, width2), BF16)
    sent = call(
        functools.partial(dispatch_kernel, front),
        [block] * pairs,
        (to_slots, source.reshape(rows, width2), arriving, sibling),
        hbm=(3,),
        scratch=[VMEM((rows, width2), BF16)],
    )
    far, near = list(range(pairs // 2, pairs)), list(range(1, pairs // 2))
    order = far[-1:] + near + far[-2::-1] + [0]
    arrived = {at: exchange(sent[at], 2 * at) if at else sent[at] for at in order}
    own, sibling = call(stage_kernel, [jax.ShapeDtypeStruct(own.shape, BF16)] * 2, (own, sibling, sent[0]), hbm=(2,))
    nodes = jax.ShapeDtypeStruct((pairs * shots, 2 * sep_n + LANES), F32)
    halves = (pairs, 2, size // 2, width2)
    first, last = order[: pairs // 2] + [0], order[pairs // 2 : -1]

    def scratch(group):
        return [
            VMEM((len(group) * size, width2), BF16),
            VMEM((len(group),) + halves[1:], BF16),
            pltpu.SemaphoreType.DMA((2 * len(group),)),
        ]

    solved, sums = call(
        functools.partial(leaf_kernel, shots, sep_n, first, pairs),
        [jax.ShapeDtypeStruct(halves, BF16), jax.ShapeDtypeStruct((2 * pairs * shots, 2 * sep_n), F32)],
        (own, sibling, *(arrived[at] for at in first)),
        hbm_out=(0,),
        scratch=scratch(first),
    )
    solved, keep, send = call(
        functools.partial(leaf_kernel, shots, sep_n, last, pairs),
        [jax.ShapeDtypeStruct(halves, BF16), nodes, jax.ShapeDtypeStruct(nodes.shape, BF16)],
        (own, sibling, *(arrived[at] for at in last), sep_code % sep_lib, sums, solved),
        smem=(2 + len(last),),
        hbm=(4 + len(last),),
        hbm_out=(0,),
        aliases={4 + len(last): 0},
        scratch=scratch(last),
    )
    back = to_pairs(solved.reshape(pairs, size, width2)).reshape(slots, width2)
    keep, arrived = path_sums(keep, send, shots, levels)
    scales = [1.0 / math.sqrt(leaves * 2 ** (level + 1)) for level in range(levels)]
    above = call(
        functools.partial(tree_kernel, scales),
        jax.ShapeDtypeStruct((2 * shots, sep_n), F32),
        (keep, arrived, sep_factors),
        cost=(1, 1),
    )
    result = call(
        functools.partial(result_kernel, shots),
        jax.ShapeDtypeStruct((leaves, shots, width2), BF16),
        (from_slots, above, back),
    )
    return result[None]


def solution(mesh):
    return jax.shard_map(
        on_device,
        mesh=mesh,
        in_specs=(
            P("panel", "leaf", None, None),
            P("panel", "leaf", None),
            P("panel", "leaf", None),
            P("panel", "leaf"),
            P("leaf", None, None, None),
            P(),
        ),
        out_specs=P("panel", "leaf", None, None),
        check_vma=False,
    )
```

```python
import functools
import math

import jax
import jax.numpy as jnp
from jax import lax
from jax.experimental import pallas as pl
from jax.experimental.pallas import tpu as pltpu
from jax.sharding import PartitionSpec as P

F32 = jnp.float32
BF16 = jnp.bfloat16
VMEM = pltpu.VMEM
LANES = 128


def around(value, axis):
    count = lax.axis_size(axis)
    return lax.ppermute(value, axis, [(at, (at + 1) % count) for at in range(count)])


def exchange(value, distance):
    pairs = [(at, at ^ distance) for at in range(lax.axis_size("leaf"))]
    return lax.ppermute(value, "leaf", pairs)


def dot(left, right):
    return jnp.dot(left, right, preferred_element_type=F32)


def one_hot(mask):
    return mask.astype(F32).astype(BF16)


def slot_kernel(shots, capacity, media_ref, to_slots_ref, from_slots_ref):
    slots, count = to_slots_ref.shape
    leaves = media_ref.shape[1]
    leaf = lax.broadcasted_iota(jnp.int32, (leaves, count), 0)
    of_row = one_hot(lax.broadcasted_iota(jnp.int32, (leaves, count), 1) // shots == leaf)
    kinds = dot(media_ref[...].astype(F32).astype(BF16), of_row).astype(jnp.int32)
    before = lax.broadcasted_iota(jnp.int32, (count, count), 0)
    later = lax.broadcasted_iota(jnp.int32, (count, count), 1)
    across = jnp.broadcast_to(kinds, (count, count))
    kinds_down = jnp.sum(jnp.where(before == later, across, 0), axis=1, keepdims=True)
    down = jnp.broadcast_to(kinds_down, (count, count))
    same = (across == down) & (before % shots == later % shots)
    rank_row = jnp.sum((same & (before < later)).astype(jnp.int32), axis=0, keepdims=True)
    rank_col = jnp.sum((same & (later < before)).astype(jnp.int32), axis=1, keepdims=True)
    shot_row = lax.broadcasted_iota(jnp.int32, (1, count), 1) % shots
    shot_col = lax.broadcasted_iota(jnp.int32, (count, 1), 0) % shots
    me = lax.axis_index("leaf")
    parity = me % 2
    row = ((kinds ^ me) * shots + shot_row) * capacity + rank_row
    col = ((kinds_down ^ parity) * shots + shot_col) * capacity + rank_col
    to_slots_ref[...] = one_hot(lax.broadcasted_iota(jnp.int32, (slots, count), 0) == row)
    from_slots_ref[...] = one_hot(lax.broadcasted_iota(jnp.int32, (count, slots), 1) == col)


def face_kernel(front, source_ref, tau_ref, out_ref, re_ref, im_ref, through_ref, sems):
    leaf_n = source_ref.shape[2] // 2
    both = 2 * front
    copies = [
        pltpu.make_async_copy(source_ref.at[:, :, pl.ds(leaf_n - both, both)], re_ref, sems.at[0]),
        pltpu.make_async_copy(source_ref.at[:, :, pl.ds(2 * leaf_n - both, both)], im_ref, sems.at[1]),
        pltpu.make_async_copy(tau_ref, through_ref, sems.at[2]),
    ]
    for copy in copies:
        copy.start()
    for copy in copies:
        copy.wait()
    face_re, face_im = re_ref[...].astype(F32), im_ref[...].astype(F32)
    tau = through_ref[...]
    first = lax.broadcasted_iota(jnp.int32, tau.shape, 2) < front
    turned = pltpu.roll(tau, front, 2)
    by_same, by_other = jnp.where(first, tau, turned), jnp.where(first, -turned, tau)
    first = lax.broadcasted_iota(jnp.int32, face_re.shape, 2) < front
    face = jnp.where(first, pltpu.roll(face_re, front, 2), face_im)
    other = jnp.where(first, pltpu.roll(face_im, front, 2), face_re)
    out_ref[...] = (by_same * face + by_other * other).reshape(out_ref.shape).astype(BF16)


def dispatch_kernel(front, pick_ref, rows_ref, arriving_ref, _, *refs):
    out_refs, rhs_ref = refs[:-1], refs[-1]
    leaf_n = rows_ref.shape[1] // 2
    rhs_ref[...] = rows_ref[...]
    for part in range(2):
        face = pl.ds((part + 1) * leaf_n - 2 * front, 2 * front)
        incoming = arriving_ref[...].astype(F32)
        lane = lax.broadcasted_iota(jnp.int32, incoming.shape, 1)
        if part == 0:
            incoming = pltpu.roll(incoming, front, 1)
        incoming = jnp.where((lane >= front) & (lax.axis_index("panel") > 0), incoming, 0.0)
        rhs_ref[:, face] = (rows_ref[:, face].astype(F32) + incoming).astype(BF16)
    size = out_refs[0].shape[0]
    send = dot(pick_ref[...], rhs_ref[...]).astype(BF16)
    for at, out_ref in enumerate(out_refs):
        out_ref[...] = send[at * size : (at + 1) * size]


def stage_kernel(own_ref, sibling_ref, _, *to_refs):
    to_refs[0][...] = own_ref[...]
    to_refs[1][...] = sibling_ref[...]


def leaf_kernel(shots, sep_n, group, pairs, own_ref, sibling_ref, *refs):
    blocks, refs = refs[: len(group)], refs[len(group) :]
    if len(refs) == 5:
        code_ref = None
        out_ref, sums_ref, rows_ref, solved_ref, sems = refs
        count = sums_ref.shape[0]
    else:
        code_ref, before_ref, _, out_ref, keep_ref, send_ref, rows_ref, solved_ref, sems = refs
        count = 2 * keep_ref.shape[0]
    leaf_n = own_ref.shape[1]
    members, _, size, _ = solved_ref.shape
    capacity = size // shots
    half = members * size
    own_pair = lax.axis_index("leaf") // 2
    bits = pairs.bit_length() - 1
    row = lax.broadcasted_iota(jnp.int32, (count, half), 0)
    place = lax.broadcasted_iota(jnp.int32, (count, half), 1)
    lead = lax.broadcasted_iota(jnp.int32, (count, LANES), 0)
    distance = jnp.zeros((count, half), jnp.int32)
    for at, block in enumerate(group):
        distance = jnp.where(place // size == at, block, distance)
    member, here, first = row < 0, lead < 0, 0
    for other in range(2):
        for level in range(bits + 1):
            nodes = 1 << bits - 1 - level if level < bits else 1
            node = (row - first) // shots + (other * nodes if level < bits else 0)
            inside = (row >= first) & (row < first + nodes * shots)
            member |= inside & (distance >> level == node)
            if not (other and level < bits):
                here |= (lead >= first) & (lead < first + shots)
            first += nodes * shots
    member = one_hot(member & (place % size // capacity == row % shots))

    copies, sums = [], [0.0, 0.0]
    for entry in range(2):
        for at in range(members):
            real = blocks[at][entry * size : (entry + 1) * size, :leaf_n]
            imag = blocks[at][entry * size : (entry + 1) * size, leaf_n:]
            first = at * size
            rows_ref[first : first + size, :leaf_n] = real
            rows_ref[first : first + size, leaf_n:] = -imag
            rows_ref[half + first : half + first + size, :leaf_n] = imag
            rows_ref[half + first : half + first + size, leaf_n:] = real
        factor = (sibling_ref if entry else own_ref)[...].reshape(2 * leaf_n, leaf_n)
        both = dot(rows_ref[...], factor).astype(BF16)
        for part in range(2):
            solved = both[part * half : (part + 1) * half]
            columns = pl.ds(part * leaf_n, leaf_n)
            for at in range(members):
                solved_ref[at, entry, :, columns] = solved[at * size : (at + 1) * size]
            sums[part] += dot(member, solved[:, :sep_n])
        for at, block in enumerate(group):
            copies.append(
                pltpu.make_async_copy(
                    solved_ref.at[at, entry], out_ref.at[own_pair ^ block, entry], sems.at[entry * members + at]
                )
            )
            copies[-1].start()
    for part in range(2):
        columns = slice(part * sep_n, (part + 1) * sep_n)
        if code_ref is None:
            sums_ref[:, columns] = sums[part]
        else:
            total = sums[part] + before_ref[:, columns]
            keep_ref[:, columns] = total[: count // 2]
            send_ref[:, columns] = total[count // 2 :].astype(BF16)
    if code_ref is not None:
        codes = jnp.where(here, code_ref[0, 0].astype(F32), 0.0)
        keep_ref[:, 2 * sep_n :] = codes[: count // 2]
        send_ref[:, 2 * sep_n :] = codes[count // 2 :].astype(BF16)
    for copy in copies:
        copy.wait()


def tree_kernel(scales, keep_ref, arrived_ref, factors_ref, out_ref):
    sep_lib, sep_n = factors_ref.shape[0], factors_ref.shape[2]
    shots = out_ref.shape[0] // 2
    sums = keep_ref[...] + arrived_ref[...].astype(F32)
    above = jnp.zeros(out_ref.shape, F32)
    for level in reversed(range(len(scales))):
        here = sums[level * shots : (level + 1) * shots]
        code = jnp.max(here[0:1, 2 * sep_n :]).astype(jnp.int32) % sep_lib
        path = jnp.concatenate([here[:, :sep_n], here[:, sep_n : 2 * sep_n]], axis=0)
        operand = (path * scales[level] - above).astype(BF16)
        factor = factors_ref[code]
        by_re, by_im = dot(operand, factor[0]), dot(operand, factor[1])
        above = jnp.concatenate([by_re[:shots] - by_im[shots:], by_im[:shots] + by_re[shots:]], axis=0)
    out_ref[...] = above


def result_kernel(shots, pick_ref, above_ref, back_ref, out_ref):
    leaves, _, width2 = out_ref.shape
    count = leaves * shots
    leaf_n = width2 // 2
    sep_n = above_ref.shape[1]
    shot = lax.broadcasted_iota(jnp.int32, (count, sep_n), 0) % shots
    for part in range(2):
        start = part * leaf_n
        solved = dot(pick_ref[...], back_ref[:, start : start + leaf_n])
        lifted = jnp.zeros((count, sep_n), F32)
        for at in range(shots):
            here = part * shots + at
            lifted = jnp.where(shot == at, above_ref[here : here + 1], lifted)
        solved = jnp.concatenate([solved[:, :sep_n] - lifted, solved[:, sep_n:]], axis=1).astype(BF16)
        out_ref[:, :, start : start + leaf_n] = solved.reshape(leaves, shots, leaf_n)


def call(kernel, out_shape, args, smem=(), hbm=(), hbm_out=(), aliases={}, scratch=(), cost=None, limit=16):
    spaces = [pltpu.SMEM if at in smem else pltpu.HBM if at in hbm else VMEM for at in range(len(args))]
    shapes = out_shape if isinstance(out_shape, list) else [out_shape]
    out_specs = [pl.BlockSpec(memory_space=pltpu.HBM if at in hbm_out else VMEM) for at in range(len(shapes))]
    return pl.pallas_call(
        kernel,
        out_shape=out_shape,
        in_specs=[pl.BlockSpec(memory_space=space) for space in spaces],
        out_specs=out_specs if isinstance(out_shape, list) else out_specs[0],
        scratch_shapes=list(scratch),
        input_output_aliases=aliases,
        cost_estimate=cost and pl.CostEstimate(flops=cost[0], bytes_accessed=cost[1], transcendentals=0),
        compiler_params=pltpu.CompilerParams(vmem_limit_bytes=int(limit * 2**20)),
    )(*args)


def to_pairs(value):
    groups = [list(range(parity, lax.axis_size("leaf"), 2)) for parity in range(2)]
    return lax.all_to_all(value, "leaf", 0, 0, tiled=True, axis_index_groups=groups)


def path_sums(keep, send, shots, levels):
    bits = levels - 1
    sizes = [1 << bits - 1 - level for level in range(bits)] + [1]
    arrived = exchange(send, 1 << bits)
    for bit in range(-1, bits - 1):
        sums = keep + arrived.astype(F32)
        mine, other, start = [], [], 0
        for level, count in enumerate(sizes):
            for node in range(count):
                rows = sums[start * shots : (start + 1) * shots]
                start += 1
                if level > bit or bit < 0:
                    mine.append(rows)
                    other.append(rows)
                else:
                    (other if node % 2 else mine).append(rows)
            if level <= bit:
                sizes[level] //= 2
        keep = jnp.concatenate(mine)
        arrived = exchange(jnp.concatenate(other).astype(BF16), 2 << bit if bit >= 0 else 1)
    return keep, arrived


def on_device(sources, transmission, media, sep_code, leaf_factors, sep_factors):
    leaves, shots, width2 = sources.shape[1:]
    leaf_n = width2 // 2
    front = transmission.shape[2] // 2
    sep_lib, sep_n = sep_factors.shape[0], sep_factors.shape[2]
    nleaf = lax.axis_size("leaf")
    levels = nleaf.bit_length() - 1
    capacity = max(2, leaves * 5 // (nleaf * 2))
    size = 2 * capacity * shots
    pairs = nleaf // 2
    slots = pairs * size
    source, tau = sources[0], transmission[0][:, None, :]
    own = leaf_factors[0]
    sibling = exchange(own, 1)

    face = jax.ShapeDtypeStruct((leaves, shots, 2 * front), BF16)
    rows = leaves * shots
    leaving = call(
        functools.partial(face_kernel, front),
        jax.ShapeDtypeStruct((rows, 2 * front), BF16),
        (source, tau),
        hbm=(0, 1),
        scratch=[VMEM(face.shape, BF16)] * 2 + [VMEM(tau.shape, F32), pltpu.SemaphoreType.DMA((3,))],
        limit=53.9,
    )
    arriving = around(leaving, "panel")
    tau_re, tau_im = tau[..., :front], tau[..., front:]
    for _ in range(lax.axis_size("panel") - 2):
        arriving = jnp.where(lax.axis_index("panel") > 0, arriving, 0).reshape(face.shape).astype(F32)
        real = arriving[..., :front] + source[..., leaf_n - front : leaf_n].astype(F32)
        imag = arriving[..., front:] + source[..., 2 * leaf_n - front :].astype(F32)
        leaving = jnp.concatenate([tau_re * real - tau_im * imag, tau_re * imag + tau_im * real], axis=-1)
        arriving = around(leaving.reshape(rows, 2 * front).astype(BF16), "panel")

    to_slots, from_slots = call(
        functools.partial(slot_kernel, shots, capacity),
        [jax.ShapeDtypeStruct((slots, rows), BF16), jax.ShapeDtypeStruct((rows, slots), BF16)],
        (media[0].reshape(1, leaves),),
    )
    block = jax.ShapeDtypeStruct((size, width2), BF16)
    sent = call(
        functools.partial(dispatch_kernel, front),
        [block] * pairs,
        (to_slots, source.reshape(rows, width2), arriving, sibling),
        hbm=(3,),
        scratch=[VMEM((rows, width2), BF16)],
    )
    far, near = list(range(pairs // 2, pairs)), list(range(1, pairs // 2))
    order = far[-1:] + near + far[-2::-1] + [0]
    arrived = {at: exchange(sent[at], 2 * at) if at else sent[at] for at in order}
    own, sibling = call(stage_kernel, [jax.ShapeDtypeStruct(own.shape, BF16)] * 2, (own, sibling, sent[0]), hbm=(2,))
    nodes = jax.ShapeDtypeStruct((pairs * shots, 2 * sep_n + LANES), F32)
    halves = (pairs, 2, size // 2, width2)
    first, last = order[: pairs // 2] + [0], order[pairs // 2 : -1]

    def scratch(group):
        return [
            VMEM((len(group) * size, width2), BF16),
            VMEM((len(group),) + halves[1:], BF16),
            pltpu.SemaphoreType.DMA((2 * len(group),)),
        ]

    solved, sums = call(
        functools.partial(leaf_kernel, shots, sep_n, first, pairs),
        [jax.ShapeDtypeStruct(halves, BF16), jax.ShapeDtypeStruct((2 * pairs * shots, 2 * sep_n), F32)],
        (own, sibling, *(arrived[at] for at in first)),
        hbm_out=(0,),
        scratch=scratch(first),
    )
    solved, keep, send = call(
        functools.partial(leaf_kernel, shots, sep_n, last, pairs),
        [jax.ShapeDtypeStruct(halves, BF16), nodes, jax.ShapeDtypeStruct(nodes.shape, BF16)],
        (own, sibling, *(arrived[at] for at in last), sep_code % sep_lib, sums, solved),
        smem=(2 + len(last),),
        hbm=(4 + len(last),),
        hbm_out=(0,),
        aliases={4 + len(last): 0},
        scratch=scratch(last),
    )
    back = to_pairs(solved.reshape(pairs, size, width2)).reshape(slots, width2)
    keep, arrived = path_sums(keep, send, shots, levels)
    scales = [1.0 / math.sqrt(leaves * 2 ** (level + 1)) for level in range(levels)]
    above = call(
        functools.partial(tree_kernel, scales),
        jax.ShapeDtypeStruct((2 * shots, sep_n), F32),
        (keep, arrived, sep_factors),
        cost=(1, 1),
    )
    result = call(
        functools.partial(result_kernel, shots),
        jax.ShapeDtypeStruct((leaves, shots, width2), BF16),
        (from_slots, above, back),
    )
    return result[None]


def solution(mesh):
    return jax.shard_map(
        on_device,
        mesh=mesh,
        in_specs=(
            P("panel", "leaf", None, None),
            P("panel", "leaf", None),
            P("panel", "leaf", None),
            P("panel", "leaf"),
            P("leaf", None, None, None),
            P(),
        ),
        out_specs=P("panel", "leaf", None, None),
        check_vma=False,
    )
```

```python
import functools
import math

import jax
import jax.numpy as jnp
from jax import lax
from jax.experimental import pallas as pl
from jax.experimental.pallas import tpu as pltpu
from jax.sharding import PartitionSpec as P

F32 = jnp.float32
BF16 = jnp.bfloat16
VMEM = pltpu.VMEM
LANES = 128


def around(value, axis):
    count = lax.axis_size(axis)
    return lax.ppermute(value, axis, [(at, (at + 1) % count) for at in range(count)])


def exchange(value, distance):
    pairs = [(at, at ^ distance) for at in range(lax.axis_size("leaf"))]
    return lax.ppermute(value, "leaf", pairs)


def dot(left, right):
    return jnp.dot(left, right, preferred_element_type=F32)


def one_hot(mask):
    return mask.astype(F32).astype(BF16)


def slot_kernel(shots, capacity, media_ref, to_slots_ref, from_slots_ref):
    slots, count = to_slots_ref.shape
    leaves = media_ref.shape[1]
    leaf = lax.broadcasted_iota(jnp.int32, (leaves, count), 0)
    of_row = one_hot(lax.broadcasted_iota(jnp.int32, (leaves, count), 1) // shots == leaf)
    kinds = dot(media_ref[...].astype(F32).astype(BF16), of_row).astype(jnp.int32)
    before = lax.broadcasted_iota(jnp.int32, (count, count), 0)
    later = lax.broadcasted_iota(jnp.int32, (count, count), 1)
    across = jnp.broadcast_to(kinds, (count, count))
    kinds_down = jnp.sum(jnp.where(before == later, across, 0), axis=1, keepdims=True)
    down = jnp.broadcast_to(kinds_down, (count, count))
    same = (across == down) & (before % shots == later % shots)
    rank_row = jnp.sum((same & (before < later)).astype(jnp.int32), axis=0, keepdims=True)
    rank_col = jnp.sum((same & (later < before)).astype(jnp.int32), axis=1, keepdims=True)
    shot_row = lax.broadcasted_iota(jnp.int32, (1, count), 1) % shots
    shot_col = lax.broadcasted_iota(jnp.int32, (count, 1), 0) % shots
    me = lax.axis_index("leaf")
    parity = me % 2
    row = ((kinds ^ me) * shots + shot_row) * capacity + rank_row
    col = ((kinds_down ^ parity) * shots + shot_col) * capacity + rank_col
    to_slots_ref[...] = one_hot(lax.broadcasted_iota(jnp.int32, (slots, count), 0) == row)
    from_slots_ref[...] = one_hot(lax.broadcasted_iota(jnp.int32, (count, slots), 1) == col)


def face_kernel(front, source_ref, tau_ref, out_ref, re_ref, im_ref, through_ref, sems):
    leaf_n = source_ref.shape[2] // 2
    both = 2 * front
    copies = [
        pltpu.make_async_copy(source_ref.at[:, :, pl.ds(leaf_n - both, both)], re_ref, sems.at[0]),
        pltpu.make_async_copy(source_ref.at[:, :, pl.ds(2 * leaf_n - both, both)], im_ref, sems.at[1]),
        pltpu.make_async_copy(tau_ref, through_ref, sems.at[2]),
    ]
    for copy in copies:
        copy.start()
    for copy in copies:
        copy.wait()
    face_re, face_im = re_ref[...].astype(F32), im_ref[...].astype(F32)
    tau = through_ref[...]
    first = lax.broadcasted_iota(jnp.int32, tau.shape, 2) < front
    turned = pltpu.roll(tau, front, 2)
    by_same, by_other = jnp.where(first, tau, turned), jnp.where(first, -turned, tau)
    first = lax.broadcasted_iota(jnp.int32, face_re.shape, 2) < front
    face = jnp.where(first, pltpu.roll(face_re, front, 2), face_im)
    other = jnp.where(first, pltpu.roll(face_im, front, 2), face_re)
    out_ref[...] = (by_same * face + by_other * other).reshape(out_ref.shape).astype(out_ref.dtype)


def dispatch_kernel(front, pick_ref, rows_ref, arriving_ref, _, *refs):
    out_refs, rhs_ref = refs[:-1], refs[-1]
    leaf_n = rows_ref.shape[1] // 2
    rhs_ref[...] = rows_ref[...]
    for part in range(2):
        face = pl.ds((part + 1) * leaf_n - 2 * front, 2 * front)
        incoming = arriving_ref[...].astype(F32)
        lane = lax.broadcasted_iota(jnp.int32, incoming.shape, 1)
        if part == 0:
            incoming = pltpu.roll(incoming, front, 1)
        incoming = jnp.where((lane >= front) & (lax.axis_index("panel") > 0), incoming, 0.0)
        rhs_ref[:, face] = (rows_ref[:, face].astype(F32) + incoming).astype(BF16)
    size = out_refs[0].shape[0]
    send = dot(pick_ref[...], rhs_ref[...]).astype(BF16)
    for at, out_ref in enumerate(out_refs):
        out_ref[...] = send[at * size : (at + 1) * size]


def stage_kernel(own_ref, sibling_ref, _, *to_refs):
    to_refs[0][...] = own_ref[...]
    to_refs[1][...] = sibling_ref[...]


def leaf_kernel(shots, sep_n, group, pairs, own_ref, sibling_ref, *refs):
    blocks, refs = refs[: len(group)], refs[len(group) :]
    if len(refs) == 5:
        code_ref = None
        out_ref, sums_ref, rows_ref, solved_ref, sems = refs
        count = sums_ref.shape[0]
    else:
        code_ref, before_ref, _, out_ref, keep_ref, send_ref, rows_ref, solved_ref, sems = refs
        count = 2 * keep_ref.shape[0]
    leaf_n = own_ref.shape[1]
    members, _, size, _ = solved_ref.shape
    capacity = size // shots
    half = members * size
    own_pair = lax.axis_index("leaf") // 2
    bits = pairs.bit_length() - 1
    row = lax.broadcasted_iota(jnp.int32, (count, half), 0)
    place = lax.broadcasted_iota(jnp.int32, (count, half), 1)
    lead = lax.broadcasted_iota(jnp.int32, (count, LANES), 0)
    distance = jnp.zeros((count, half), jnp.int32)
    for at, block in enumerate(group):
        distance = jnp.where(place // size == at, block, distance)
    member, here, first = row < 0, lead < 0, 0
    for other in range(2):
        for level in range(bits + 1):
            nodes = 1 << bits - 1 - level if level < bits else 1
            node = (row - first) // shots + (other * nodes if level < bits else 0)
            inside = (row >= first) & (row < first + nodes * shots)
            member |= inside & (distance >> level == node)
            if not (other and level < bits):
                here |= (lead >= first) & (lead < first + shots)
            first += nodes * shots
    member = one_hot(member & (place % size // capacity == row % shots))

    copies, sums = [], [0.0, 0.0]
    for entry in range(2):
        for at in range(members):
            real = blocks[at][entry * size : (entry + 1) * size, :leaf_n]
            imag = blocks[at][entry * size : (entry + 1) * size, leaf_n:]
            first = at * size
            rows_ref[first : first + size, :leaf_n] = real
            rows_ref[first : first + size, leaf_n:] = -imag
            rows_ref[half + first : half + first + size, :leaf_n] = imag
            rows_ref[half + first : half + first + size, leaf_n:] = real
        factor = (sibling_ref if entry else own_ref)[...].reshape(2 * leaf_n, leaf_n)
        both = dot(rows_ref[...], factor).astype(BF16)
        for part in range(2):
            solved = both[part * half : (part + 1) * half]
            columns = pl.ds(part * leaf_n, leaf_n)
            for at in range(members):
                solved_ref[at, entry, :, columns] = solved[at * size : (at + 1) * size]
            sums[part] += dot(member, solved[:, :sep_n])
        for at, block in enumerate(group):
            copies.append(
                pltpu.make_async_copy(
                    solved_ref.at[at, entry], out_ref.at[own_pair ^ block, entry], sems.at[entry * members + at]
                )
            )
            copies[-1].start()
    for part in range(2):
        columns = slice(part * sep_n, (part + 1) * sep_n)
        if code_ref is None:
            sums_ref[:, columns] = sums[part]
        else:
            total = sums[part] + before_ref[:, columns]
            keep_ref[:, columns] = total[: count // 2]
            send_ref[:, columns] = total[count // 2 :].astype(send_ref.dtype)
    if code_ref is not None:
        codes = jnp.where(here, code_ref[0, 0].astype(F32), 0.0)
        keep_ref[:, 2 * sep_n :] = codes[: count // 2]
        send_ref[:, 2 * sep_n :] = codes[count // 2 :].astype(send_ref.dtype)
    for copy in copies:
        copy.wait()


def tree_kernel(scales, keep_ref, arrived_ref, factors_ref, out_ref):
    sep_lib, sep_n = factors_ref.shape[0], factors_ref.shape[2]
    shots = out_ref.shape[0] // 2
    sums = keep_ref[...] + arrived_ref[...].astype(F32)
    above = jnp.zeros(out_ref.shape, F32)
    for level in reversed(range(len(scales))):
        here = sums[level * shots : (level + 1) * shots]
        code = jnp.max(here[0:1, 2 * sep_n :]).astype(jnp.int32) % sep_lib
        path = jnp.concatenate([here[:, :sep_n], here[:, sep_n : 2 * sep_n]], axis=0)
        operand = (path * scales[level] - above).astype(BF16)
        factor = factors_ref[code]
        by_re, by_im = dot(operand, factor[0]), dot(operand, factor[1])
        above = jnp.concatenate([by_re[:shots] - by_im[shots:], by_im[:shots] + by_re[shots:]], axis=0)
    out_ref[...] = above


def result_kernel(shots, pick_ref, above_ref, back_ref, out_ref):
    leaves, _, width2 = out_ref.shape
    count = leaves * shots
    leaf_n = width2 // 2
    sep_n = above_ref.shape[1]
    shot = lax.broadcasted_iota(jnp.int32, (count, sep_n), 0) % shots
    for part in range(2):
        start = part * leaf_n
        solved = dot(pick_ref[...], back_ref[:, start : start + leaf_n])
        lifted = jnp.zeros((count, sep_n), F32)
        for at in range(shots):
            here = part * shots + at
            lifted = jnp.where(shot == at, above_ref[here : here + 1], lifted)
        solved = jnp.concatenate([solved[:, :sep_n] - lifted, solved[:, sep_n:]], axis=1).astype(BF16)
        out_ref[:, :, start : start + leaf_n] = solved.reshape(leaves, shots, leaf_n)


def call(kernel, out_shape, args, smem=(), hbm=(), hbm_out=(), aliases={}, scratch=(), cost=None, limit=16):
    spaces = [pltpu.SMEM if at in smem else pltpu.HBM if at in hbm else VMEM for at in range(len(args))]
    shapes = out_shape if isinstance(out_shape, list) else [out_shape]
    out_specs = [pl.BlockSpec(memory_space=pltpu.HBM if at in hbm_out else VMEM) for at in range(len(shapes))]
    return pl.pallas_call(
        kernel,
        out_shape=out_shape,
        in_specs=[pl.BlockSpec(memory_space=space) for space in spaces],
        out_specs=out_specs if isinstance(out_shape, list) else out_specs[0],
        scratch_shapes=list(scratch),
        input_output_aliases=aliases,
        cost_estimate=cost and pl.CostEstimate(flops=cost[0], bytes_accessed=cost[1], transcendentals=0),
        compiler_params=pltpu.CompilerParams(vmem_limit_bytes=int(limit * 2**20)),
    )(*args)


def to_pairs(value):
    groups = [list(range(parity, lax.axis_size("leaf"), 2)) for parity in range(2)]
    return lax.all_to_all(value, "leaf", 0, 0, tiled=True, axis_index_groups=groups)


def path_sums(keep, send, shots, levels):
    bits = levels - 1
    sizes = [1 << bits - 1 - level for level in range(bits)] + [1]
    arrived = exchange(send, 1 << bits)
    for bit in range(-1, bits - 1):
        sums = keep + arrived.astype(F32)
        mine, other, start = [], [], 0
        for level, count in enumerate(sizes):
            for node in range(count):
                rows = sums[start * shots : (start + 1) * shots]
                start += 1
                if level > bit or bit < 0:
                    mine.append(rows)
                    other.append(rows)
                else:
                    (other if node % 2 else mine).append(rows)
            if level <= bit:
                sizes[level] //= 2
        keep = jnp.concatenate(mine)
        other = jnp.concatenate(other)
        arrived = exchange(other, 2 << bit) if bit >= 0 else exchange(other.astype(BF16), 1)
    return keep, arrived


def on_device(sources, transmission, media, sep_code, leaf_factors, sep_factors):
    leaves, shots, width2 = sources.shape[1:]
    leaf_n = width2 // 2
    front = transmission.shape[2] // 2
    sep_lib, sep_n = sep_factors.shape[0], sep_factors.shape[2]
    nleaf = lax.axis_size("leaf")
    levels = nleaf.bit_length() - 1
    capacity = max(2, leaves * 5 // (nleaf * 2))
    size = 2 * capacity * shots
    pairs = nleaf // 2
    slots = pairs * size
    source, tau = sources[0], transmission[0][:, None, :]
    own = leaf_factors[0]
    sibling = exchange(own, 1)

    face = jax.ShapeDtypeStruct((leaves, shots, 2 * front), BF16)
    rows = leaves * shots
    leaving = call(
        functools.partial(face_kernel, front),
        jax.ShapeDtypeStruct((rows, 2 * front), BF16),
        (source, tau),
        hbm=(0, 1),
        scratch=[VMEM(face.shape, BF16)] * 2 + [VMEM(tau.shape, F32), pltpu.SemaphoreType.DMA((3,))],
        limit=53.9,
    )
    arriving = around(leaving, "panel")
    tau_re, tau_im = tau[..., :front], tau[..., front:]
    for _ in range(lax.axis_size("panel") - 2):
        arriving = jnp.where(lax.axis_index("panel") > 0, arriving, 0).reshape(face.shape).astype(F32)
        real = arriving[..., :front] + source[..., leaf_n - front : leaf_n].astype(F32)
        imag = arriving[..., front:] + source[..., 2 * leaf_n - front :].astype(F32)
        leaving = jnp.concatenate([tau_re * real - tau_im * imag, tau_re * imag + tau_im * real], axis=-1)
        arriving = around(leaving.reshape(rows, 2 * front).astype(BF16), "panel")

    to_slots, from_slots = call(
        functools.partial(slot_kernel, shots, capacity),
        [jax.ShapeDtypeStruct((slots, rows), BF16), jax.ShapeDtypeStruct((rows, slots), BF16)],
        (media[0].reshape(1, leaves),),
    )
    block = jax.ShapeDtypeStruct((size, width2), BF16)
    sent = call(
        functools.partial(dispatch_kernel, front),
        [block] * pairs,
        (to_slots, source.reshape(rows, width2), arriving, sibling),
        hbm=(3,),
        scratch=[VMEM((rows, width2), BF16)],
    )
    far, near = list(range(pairs // 2, pairs)), list(range(1, pairs // 2))
    order = far[-1:] + near + far[-2::-1] + [0]
    arrived = {at: exchange(sent[at], 2 * at) if at else sent[at] for at in order}
    own, sibling = call(stage_kernel, [jax.ShapeDtypeStruct(own.shape, BF16)] * 2, (own, sibling, sent[0]), hbm=(2,))
    nodes = jax.ShapeDtypeStruct((pairs * shots, 2 * sep_n + LANES), F32)
    halves = (pairs, 2, size // 2, width2)
    first, last = order[: pairs // 2] + [0], order[pairs // 2 : -1]

    def scratch(group):
        return [
            VMEM((len(group) * size, width2), BF16),
            VMEM((len(group),) + halves[1:], BF16),
            pltpu.SemaphoreType.DMA((2 * len(group),)),
        ]

    solved, sums = call(
        functools.partial(leaf_kernel, shots, sep_n, first, pairs),
        [jax.ShapeDtypeStruct(halves, BF16), jax.ShapeDtypeStruct((2 * pairs * shots, 2 * sep_n), F32)],
        (own, sibling, *(arrived[at] for at in first)),
        hbm_out=(0,),
        scratch=scratch(first),
    )
    solved, keep, send = call(
        functools.partial(leaf_kernel, shots, sep_n, last, pairs),
        [jax.ShapeDtypeStruct(halves, BF16), nodes, nodes],
        (own, sibling, *(arrived[at] for at in last), sep_code % sep_lib, sums, solved),
        smem=(2 + len(last),),
        hbm=(4 + len(last),),
        hbm_out=(0,),
        aliases={4 + len(last): 0},
        scratch=scratch(last),
    )
    back = to_pairs(solved.reshape(pairs, size, width2)).reshape(slots, width2)
    keep, arrived = path_sums(keep, send, shots, levels)
    scales = [1.0 / math.sqrt(leaves * 2 ** (level + 1)) for level in range(levels)]
    above = call(
        functools.partial(tree_kernel, scales),
        jax.ShapeDtypeStruct((2 * shots, sep_n), F32),
        (keep, arrived, sep_factors),
        cost=(1, 1),
    )
    result = call(
        functools.partial(result_kernel, shots),
        jax.ShapeDtypeStruct((leaves, shots, width2), BF16),
        (from_slots, above, back),
    )
    return result[None]


def solution(mesh):
    return jax.shard_map(
        on_device,
        mesh=mesh,
        in_specs=(
            P("panel", "leaf", None, None),
            P("panel", "leaf", None),
            P("panel", "leaf", None),
            P("panel", "leaf"),
            P("leaf", None, None, None),
            P(),
        ),
        out_specs=P("panel", "leaf", None, None),
        check_vma=False,
    )
```

```python
import functools
import math

import jax
import jax.numpy as jnp
from jax import lax
from jax.experimental import pallas as pl
from jax.experimental.pallas import tpu as pltpu
from jax.sharding import PartitionSpec as P

F32 = jnp.float32
BF16 = jnp.bfloat16
VMEM = pltpu.VMEM
LANES = 128


def around(value, axis):
    count = lax.axis_size(axis)
    return lax.ppermute(value, axis, [(at, (at + 1) % count) for at in range(count)])


def exchange(value, distance):
    pairs = [(at, at ^ distance) for at in range(lax.axis_size("leaf"))]
    return lax.ppermute(value, "leaf", pairs)


def dot(left, right):
    return jnp.dot(left, right, preferred_element_type=F32)


def one_hot(mask):
    return mask.astype(F32).astype(BF16)


def slot_kernel(shots, capacity, media_ref, to_slots_ref, from_slots_ref):
    slots, count = to_slots_ref.shape
    leaves = media_ref.shape[1]
    leaf = lax.broadcasted_iota(jnp.int32, (leaves, count), 0)
    of_row = one_hot(lax.broadcasted_iota(jnp.int32, (leaves, count), 1) // shots == leaf)
    kinds = dot(media_ref[...].astype(F32).astype(BF16), of_row).astype(jnp.int32)
    before = lax.broadcasted_iota(jnp.int32, (count, count), 0)
    later = lax.broadcasted_iota(jnp.int32, (count, count), 1)
    across = jnp.broadcast_to(kinds, (count, count))
    kinds_down = jnp.sum(jnp.where(before == later, across, 0), axis=1, keepdims=True)
    down = jnp.broadcast_to(kinds_down, (count, count))
    same = (across == down) & (before % shots == later % shots)
    rank_row = jnp.sum((same & (before < later)).astype(jnp.int32), axis=0, keepdims=True)
    rank_col = jnp.sum((same & (later < before)).astype(jnp.int32), axis=1, keepdims=True)
    shot_row = lax.broadcasted_iota(jnp.int32, (1, count), 1) % shots
    shot_col = lax.broadcasted_iota(jnp.int32, (count, 1), 0) % shots
    me = lax.axis_index("leaf")
    parity = me % 2
    row = ((kinds ^ me) * shots + shot_row) * capacity + rank_row
    col = ((kinds_down ^ parity) * shots + shot_col) * capacity + rank_col
    to_slots_ref[...] = one_hot(lax.broadcasted_iota(jnp.int32, (slots, count), 0) == row)
    from_slots_ref[...] = one_hot(lax.broadcasted_iota(jnp.int32, (count, slots), 1) == col)


def face_kernel(front, source_ref, tau_ref, out_ref, re_ref, im_ref, through_ref, sems):
    leaf_n = source_ref.shape[2] // 2
    both = 2 * front
    copies = [
        pltpu.make_async_copy(source_ref.at[:, :, pl.ds(leaf_n - both, both)], re_ref, sems.at[0]),
        pltpu.make_async_copy(source_ref.at[:, :, pl.ds(2 * leaf_n - both, both)], im_ref, sems.at[1]),
        pltpu.make_async_copy(tau_ref, through_ref, sems.at[2]),
    ]
    for copy in copies:
        copy.start()
    for copy in copies:
        copy.wait()
    face_re, face_im = re_ref[...].astype(F32), im_ref[...].astype(F32)
    tau = through_ref[...]
    first = lax.broadcasted_iota(jnp.int32, tau.shape, 2) < front
    turned = pltpu.roll(tau, front, 2)
    by_same, by_other = jnp.where(first, tau, turned), jnp.where(first, -turned, tau)
    first = lax.broadcasted_iota(jnp.int32, face_re.shape, 2) < front
    face = jnp.where(first, pltpu.roll(face_re, front, 2), face_im)
    other = jnp.where(first, pltpu.roll(face_im, front, 2), face_re)
    out_ref[...] = (by_same * face + by_other * other).reshape(out_ref.shape).astype(out_ref.dtype)


def dispatch_kernel(front, pick_ref, rows_ref, arriving_ref, _, *refs):
    out_refs, rhs_ref = refs[:-1], refs[-1]
    leaf_n = rows_ref.shape[1] // 2
    rhs_ref[...] = rows_ref[...]
    for part in range(2):
        face = pl.ds((part + 1) * leaf_n - 2 * front, 2 * front)
        incoming = arriving_ref[...].astype(F32)
        lane = lax.broadcasted_iota(jnp.int32, incoming.shape, 1)
        if part == 0:
            incoming = pltpu.roll(incoming, front, 1)
        incoming = jnp.where((lane >= front) & (lax.axis_index("panel") > 0), incoming, 0.0)
        rhs_ref[:, face] = (rows_ref[:, face].astype(F32) + incoming).astype(BF16)
    size = out_refs[0].shape[0]
    send = dot(pick_ref[...], rhs_ref[...]).astype(BF16)
    for at, out_ref in enumerate(out_refs):
        out_ref[...] = send[at * size : (at + 1) * size]


def stage_kernel(own_ref, sibling_ref, _, *to_refs):
    to_refs[0][...] = own_ref[...]
    to_refs[1][...] = sibling_ref[...]


def leaf_kernel(shots, sep_n, group, pairs, own_ref, sibling_ref, *refs):
    blocks, refs = refs[: len(group)], refs[len(group) :]
    if len(refs) == 5:
        code_ref = None
        out_ref, sums_ref, rows_ref, solved_ref, sems = refs
        count = sums_ref.shape[0]
    else:
        code_ref, before_ref, _, out_ref, keep_ref, send_ref, rows_ref, solved_ref, sems = refs
        count = 2 * keep_ref.shape[0]
    leaf_n = own_ref.shape[1]
    members, _, size, _ = solved_ref.shape
    capacity = size // shots
    half = members * size
    own_pair = lax.axis_index("leaf") // 2
    bits = pairs.bit_length() - 1
    row = lax.broadcasted_iota(jnp.int32, (count, half), 0)
    place = lax.broadcasted_iota(jnp.int32, (count, half), 1)
    lead = lax.broadcasted_iota(jnp.int32, (count, LANES), 0)
    distance = jnp.zeros((count, half), jnp.int32)
    for at, block in enumerate(group):
        distance = jnp.where(place // size == at, block, distance)
    member, here, first = row < 0, lead < 0, 0
    for other in range(2):
        for level in range(bits + 1):
            nodes = 1 << bits - 1 - level if level < bits else 1
            node = (row - first) // shots + (other * nodes if level < bits else 0)
            inside = (row >= first) & (row < first + nodes * shots)
            member |= inside & (distance >> level == node)
            if not (other and level < bits):
                here |= (lead >= first) & (lead < first + shots)
            first += nodes * shots
    member = one_hot(member & (place % size // capacity == row % shots))

    copies, sums = [], [0.0, 0.0]
    for entry in range(2):
        for at in range(members):
            real = blocks[at][entry * size : (entry + 1) * size, :leaf_n]
            imag = blocks[at][entry * size : (entry + 1) * size, leaf_n:]
            first = at * size
            rows_ref[first : first + size, :leaf_n] = real
            rows_ref[first : first + size, leaf_n:] = -imag
            rows_ref[half + first : half + first + size, :leaf_n] = imag
            rows_ref[half + first : half + first + size, leaf_n:] = real
        factor = (sibling_ref if entry else own_ref)[...].reshape(2 * leaf_n, leaf_n)
        both = dot(rows_ref[...], factor).astype(BF16)
        for part in range(2):
            solved = both[part * half : (part + 1) * half]
            columns = pl.ds(part * leaf_n, leaf_n)
            for at in range(members):
                solved_ref[at, entry, :, columns] = solved[at * size : (at + 1) * size]
        for at, block in enumerate(group):
            copies.append(
                pltpu.make_async_copy(
                    solved_ref.at[at, entry], out_ref.at[own_pair ^ block, entry], sems.at[entry * members + at]
                )
            )
            copies[-1].start()
        for part in range(2):
            sums[part] += dot(member, both[part * half : (part + 1) * half, :sep_n])
    for part in range(2):
        columns = slice(part * sep_n, (part + 1) * sep_n)
        if code_ref is None:
            sums_ref[:, columns] = sums[part]
        else:
            total = sums[part] + before_ref[:, columns]
            keep_ref[:, columns] = total[: count // 2]
            send_ref[:, columns] = total[count // 2 :].astype(send_ref.dtype)
    if code_ref is not None:
        codes = jnp.where(here, code_ref[0, 0].astype(F32), 0.0)
        keep_ref[:, 2 * sep_n :] = codes[: count // 2]
        send_ref[:, 2 * sep_n :] = codes[count // 2 :].astype(send_ref.dtype)
    for copy in copies:
        copy.wait()


def tree_kernel(scales, keep_ref, arrived_ref, factors_ref, out_ref):
    sep_lib, sep_n = factors_ref.shape[0], factors_ref.shape[2]
    shots = out_ref.shape[0] // 2
    sums = keep_ref[...] + arrived_ref[...].astype(F32)
    above = jnp.zeros(out_ref.shape, F32)
    for level in reversed(range(len(scales))):
        here = sums[level * shots : (level + 1) * shots]
        code = jnp.max(here[0:1, 2 * sep_n :]).astype(jnp.int32) % sep_lib
        path = jnp.concatenate([here[:, :sep_n], here[:, sep_n : 2 * sep_n]], axis=0)
        operand = (path * scales[level] - above).astype(BF16)
        factor = factors_ref[code]
        by_re, by_im = dot(operand, factor[0]), dot(operand, factor[1])
        above = jnp.concatenate([by_re[:shots] - by_im[shots:], by_im[:shots] + by_re[shots:]], axis=0)
    out_ref[...] = above


def result_kernel(shots, pick_ref, above_ref, back_ref, out_ref):
    leaves, _, width2 = out_ref.shape
    count = leaves * shots
    leaf_n = width2 // 2
    sep_n = above_ref.shape[1]
    shot = lax.broadcasted_iota(jnp.int32, (count, sep_n), 0) % shots
    for part in range(2):
        start = part * leaf_n
        solved = dot(pick_ref[...], back_ref[:, start : start + leaf_n])
        lifted = jnp.zeros((count, sep_n), F32)
        for at in range(shots):
            here = part * shots + at
            lifted = jnp.where(shot == at, above_ref[here : here + 1], lifted)
        solved = jnp.concatenate([solved[:, :sep_n] - lifted, solved[:, sep_n:]], axis=1).astype(BF16)
        out_ref[:, :, start : start + leaf_n] = solved.reshape(leaves, shots, leaf_n)


def call(kernel, out_shape, args, smem=(), hbm=(), hbm_out=(), aliases={}, scratch=(), cost=None, limit=16):
    spaces = [pltpu.SMEM if at in smem else pltpu.HBM if at in hbm else VMEM for at in range(len(args))]
    shapes = out_shape if isinstance(out_shape, list) else [out_shape]
    out_specs = [pl.BlockSpec(memory_space=pltpu.HBM if at in hbm_out else VMEM) for at in range(len(shapes))]
    return pl.pallas_call(
        kernel,
        out_shape=out_shape,
        in_specs=[pl.BlockSpec(memory_space=space) for space in spaces],
        out_specs=out_specs if isinstance(out_shape, list) else out_specs[0],
        scratch_shapes=list(scratch),
        input_output_aliases=aliases,
        cost_estimate=cost and pl.CostEstimate(flops=cost[0], bytes_accessed=cost[1], transcendentals=0),
        compiler_params=pltpu.CompilerParams(vmem_limit_bytes=int(limit * 2**20)),
    )(*args)


def to_pairs(value):
    groups = [list(range(parity, lax.axis_size("leaf"), 2)) for parity in range(2)]
    return lax.all_to_all(value, "leaf", 0, 0, tiled=True, axis_index_groups=groups)


def path_sums(keep, send, shots, levels):
    bits = levels - 1
    sizes = [1 << bits - 1 - level for level in range(bits)] + [1]
    arrived = exchange(send, 1 << bits)
    for bit in range(-1, bits - 1):
        sums = keep + arrived.astype(F32)
        mine, other, start = [], [], 0
        for level, count in enumerate(sizes):
            for node in range(count):
                rows = sums[start * shots : (start + 1) * shots]
                start += 1
                if level > bit or bit < 0:
                    mine.append(rows)
                    other.append(rows)
                else:
                    (other if node % 2 else mine).append(rows)
            if level <= bit:
                sizes[level] //= 2
        keep = jnp.concatenate(mine)
        other = jnp.concatenate(other)
        arrived = exchange(other, 2 << bit) if bit >= 0 else exchange(other.astype(BF16), 1)
    return keep, arrived


def on_device(sources, transmission, media, sep_code, leaf_factors, sep_factors):
    leaves, shots, width2 = sources.shape[1:]
    leaf_n = width2 // 2
    front = transmission.shape[2] // 2
    sep_lib, sep_n = sep_factors.shape[0], sep_factors.shape[2]
    nleaf = lax.axis_size("leaf")
    levels = nleaf.bit_length() - 1
    capacity = max(2, leaves * 5 // (nleaf * 2))
    size = 2 * capacity * shots
    pairs = nleaf // 2
    slots = pairs * size
    source, tau = sources[0], transmission[0][:, None, :]
    own = leaf_factors[0]
    sibling = exchange(own, 1)

    face = jax.ShapeDtypeStruct((leaves, shots, 2 * front), BF16)
    rows = leaves * shots
    leaving = call(
        functools.partial(face_kernel, front),
        jax.ShapeDtypeStruct((rows, 2 * front), BF16),
        (source, tau),
        hbm=(0, 1),
        scratch=[VMEM(face.shape, BF16)] * 2 + [VMEM(tau.shape, F32), pltpu.SemaphoreType.DMA((3,))],
        limit=53.9,
    )
    arriving = around(leaving, "panel")
    tau_re, tau_im = tau[..., :front], tau[..., front:]
    for _ in range(lax.axis_size("panel") - 2):
        arriving = jnp.where(lax.axis_index("panel") > 0, arriving, 0).reshape(face.shape).astype(F32)
        real = arriving[..., :front] + source[..., leaf_n - front : leaf_n].astype(F32)
        imag = arriving[..., front:] + source[..., 2 * leaf_n - front :].astype(F32)
        leaving = jnp.concatenate([tau_re * real - tau_im * imag, tau_re * imag + tau_im * real], axis=-1)
        arriving = around(leaving.reshape(rows, 2 * front).astype(BF16), "panel")

    to_slots, from_slots = call(
        functools.partial(slot_kernel, shots, capacity),
        [jax.ShapeDtypeStruct((slots, rows), BF16), jax.ShapeDtypeStruct((rows, slots), BF16)],
        (media[0].reshape(1, leaves),),
    )
    block = jax.ShapeDtypeStruct((size, width2), BF16)
    sent = call(
        functools.partial(dispatch_kernel, front),
        [block] * pairs,
        (to_slots, source.reshape(rows, width2), arriving, sibling),
        hbm=(3,),
        scratch=[VMEM((rows, width2), BF16)],
    )
    far, near = list(range(pairs // 2, pairs)), list(range(1, pairs // 2))
    order = far[-1:] + near + far[-2::-1] + [0]
    arrived = {at: exchange(sent[at], 2 * at) if at else sent[at] for at in order}
    own, sibling = call(stage_kernel, [jax.ShapeDtypeStruct(own.shape, BF16)] * 2, (own, sibling, sent[0]), hbm=(2,))
    nodes = jax.ShapeDtypeStruct((pairs * shots, 2 * sep_n + LANES), F32)
    halves = (pairs, 2, size // 2, width2)
    first, last = order[: pairs // 2] + [0], order[pairs // 2 : -1]

    def scratch(group):
        return [
            VMEM((len(group) * size, width2), BF16),
            VMEM((len(group),) + halves[1:], BF16),
            pltpu.SemaphoreType.DMA((2 * len(group),)),
        ]

    solved, sums = call(
        functools.partial(leaf_kernel, shots, sep_n, first, pairs),
        [jax.ShapeDtypeStruct(halves, BF16), jax.ShapeDtypeStruct((2 * pairs * shots, 2 * sep_n), F32)],
        (own, sibling, *(arrived[at] for at in first)),
        hbm_out=(0,),
        scratch=scratch(first),
    )
    solved, keep, send = call(
        functools.partial(leaf_kernel, shots, sep_n, last, pairs),
        [jax.ShapeDtypeStruct(halves, BF16), nodes, nodes],
        (own, sibling, *(arrived[at] for at in last), sep_code % sep_lib, sums, solved),
        smem=(2 + len(last),),
        hbm=(4 + len(last),),
        hbm_out=(0,),
        aliases={4 + len(last): 0},
        scratch=scratch(last),
    )
    back = to_pairs(solved.reshape(pairs, size, width2)).reshape(slots, width2)
    keep, arrived = path_sums(keep, send, shots, levels)
    scales = [1.0 / math.sqrt(leaves * 2 ** (level + 1)) for level in range(levels)]
    above = call(
        functools.partial(tree_kernel, scales),
        jax.ShapeDtypeStruct((2 * shots, sep_n), F32),
        (keep, arrived, sep_factors),
        cost=(1, 1),
    )
    result = call(
        functools.partial(result_kernel, shots),
        jax.ShapeDtypeStruct((leaves, shots, width2), BF16),
        (from_slots, above, back),
    )
    return result[None]


def solution(mesh):
    return jax.shard_map(
        on_device,
        mesh=mesh,
        in_specs=(
            P("panel", "leaf", None, None),
            P("panel", "leaf", None),
            P("panel", "leaf", None),
            P("panel", "leaf"),
            P("leaf", None, None, None),
            P(),
        ),
        out_specs=P("panel", "leaf", None, None),
        check_vma=False,
    )
```

```python
import functools
import math

import jax
import jax.numpy as jnp
from jax import lax
from jax.experimental import pallas as pl
from jax.experimental.pallas import tpu as pltpu
from jax.sharding import PartitionSpec as P

F32 = jnp.float32
BF16 = jnp.bfloat16
VMEM = pltpu.VMEM
LANES = 128


def around(value, axis):
    count = lax.axis_size(axis)
    return lax.ppermute(value, axis, [(at, (at + 1) % count) for at in range(count)])


def exchange(value, distance):
    pairs = [(at, at ^ distance) for at in range(lax.axis_size("leaf"))]
    return lax.ppermute(value, "leaf", pairs)


def dot(left, right):
    return jnp.dot(left, right, preferred_element_type=F32)


def one_hot(mask):
    return mask.astype(F32).astype(BF16)


def slot_kernel(shots, capacity, media_ref, to_slots_ref, from_slots_ref):
    slots, count = to_slots_ref.shape
    leaves = media_ref.shape[1]
    leaf = lax.broadcasted_iota(jnp.int32, (leaves, count), 0)
    of_row = one_hot(lax.broadcasted_iota(jnp.int32, (leaves, count), 1) // shots == leaf)
    kinds = dot(media_ref[...].astype(F32).astype(BF16), of_row).astype(jnp.int32)
    before = lax.broadcasted_iota(jnp.int32, (count, count), 0)
    later = lax.broadcasted_iota(jnp.int32, (count, count), 1)
    across = jnp.broadcast_to(kinds, (count, count))
    kinds_down = jnp.sum(jnp.where(before == later, across, 0), axis=1, keepdims=True)
    down = jnp.broadcast_to(kinds_down, (count, count))
    same = (across == down) & (before % shots == later % shots)
    rank_row = jnp.sum((same & (before < later)).astype(jnp.int32), axis=0, keepdims=True)
    rank_col = jnp.sum((same & (later < before)).astype(jnp.int32), axis=1, keepdims=True)
    shot_row = lax.broadcasted_iota(jnp.int32, (1, count), 1) % shots
    shot_col = lax.broadcasted_iota(jnp.int32, (count, 1), 0) % shots
    me = lax.axis_index("leaf")
    parity = me % 2
    row = ((kinds ^ me) * shots + shot_row) * capacity + rank_row
    col = ((kinds_down ^ parity) * shots + shot_col) * capacity + rank_col
    to_slots_ref[...] = one_hot(lax.broadcasted_iota(jnp.int32, (slots, count), 0) == row)
    from_slots_ref[...] = one_hot(lax.broadcasted_iota(jnp.int32, (count, slots), 1) == col)


def face_kernel(front, source_ref, tau_ref, out_ref, re_ref, im_ref, through_ref, sems):
    leaf_n = source_ref.shape[2] // 2
    both = 2 * front
    copies = [
        pltpu.make_async_copy(source_ref.at[:, :, pl.ds(leaf_n - both, both)], re_ref, sems.at[0]),
        pltpu.make_async_copy(source_ref.at[:, :, pl.ds(2 * leaf_n - both, both)], im_ref, sems.at[1]),
        pltpu.make_async_copy(tau_ref, through_ref, sems.at[2]),
    ]
    for copy in copies:
        copy.start()
    for copy in copies:
        copy.wait()
    face_re, face_im = re_ref[...].astype(F32), im_ref[...].astype(F32)
    tau = through_ref[...]
    first = lax.broadcasted_iota(jnp.int32, tau.shape, 2) < front
    turned = pltpu.roll(tau, front, 2)
    by_same, by_other = jnp.where(first, tau, turned), jnp.where(first, -turned, tau)
    first = lax.broadcasted_iota(jnp.int32, face_re.shape, 2) < front
    face = jnp.where(first, pltpu.roll(face_re, front, 2), face_im)
    other = jnp.where(first, pltpu.roll(face_im, front, 2), face_re)
    out_ref[...] = (by_same * face + by_other * other).reshape(out_ref.shape).astype(out_ref.dtype)


def dispatch_kernel(front, pick_ref, rows_ref, arriving_ref, _, *refs):
    out_refs, rhs_ref = refs[:-1], refs[-1]
    leaf_n = rows_ref.shape[1] // 2
    rhs_ref[...] = rows_ref[...]
    for part in range(2):
        face = pl.ds((part + 1) * leaf_n - 2 * front, 2 * front)
        incoming = arriving_ref[...].astype(F32)
        lane = lax.broadcasted_iota(jnp.int32, incoming.shape, 1)
        if part == 0:
            incoming = pltpu.roll(incoming, front, 1)
        incoming = jnp.where((lane >= front) & (lax.axis_index("panel") > 0), incoming, 0.0)
        rhs_ref[:, face] = (rows_ref[:, face].astype(F32) + incoming).astype(BF16)
    size = out_refs[0].shape[0]
    send = dot(pick_ref[...], rhs_ref[...]).astype(BF16)
    for at, out_ref in enumerate(out_refs):
        out_ref[...] = send[at * size : (at + 1) * size]


def stage_kernel(own_ref, sibling_ref, _, *to_refs):
    to_refs[0][...] = own_ref[...]
    to_refs[1][...] = sibling_ref[...]


def leaf_kernel(shots, sep_n, group, pairs, own_ref, sibling_ref, *refs):
    blocks, refs = refs[: len(group)], refs[len(group) :]
    if len(refs) == 5:
        code_ref = None
        out_ref, sums_ref, rows_ref, solved_ref, sems = refs
        count = sums_ref.shape[0]
    else:
        code_ref, before_ref, _, out_ref, keep_ref, send_ref, rows_ref, solved_ref, sems = refs
        count = 2 * keep_ref.shape[0]
    leaf_n = own_ref.shape[1]
    members, _, size, _ = solved_ref.shape
    capacity = size // shots
    half = members * size
    own_pair = lax.axis_index("leaf") // 2
    bits = pairs.bit_length() - 1
    row = lax.broadcasted_iota(jnp.int32, (count, half), 0)
    place = lax.broadcasted_iota(jnp.int32, (count, half), 1)
    lead = lax.broadcasted_iota(jnp.int32, (count, LANES), 0)
    distance = jnp.zeros((count, half), jnp.int32)
    for at, block in enumerate(group):
        distance = jnp.where(place // size == at, block, distance)
    member, here, first = row < 0, lead < 0, 0
    for other in range(2):
        for level in range(bits + 1):
            nodes = 1 << bits - 1 - level if level < bits else 1
            node = (row - first) // shots + (other * nodes if level < bits else 0)
            inside = (row >= first) & (row < first + nodes * shots)
            member |= inside & (distance >> level == node)
            if not (other and level < bits):
                here |= (lead >= first) & (lead < first + shots)
            first += nodes * shots
    member = one_hot(member & (place % size // capacity == row % shots))

    copies, sums = [], [0.0, 0.0]
    for entry in range(2):
        for at in range(members):
            real = blocks[at][entry * size : (entry + 1) * size, :leaf_n]
            imag = blocks[at][entry * size : (entry + 1) * size, leaf_n:]
            first = at * size
            rows_ref[first : first + size, :leaf_n] = real
            rows_ref[first : first + size, leaf_n:] = -imag
            rows_ref[half + first : half + first + size, :leaf_n] = imag
            rows_ref[half + first : half + first + size, leaf_n:] = real
        factor = (sibling_ref if entry else own_ref)[...].reshape(2 * leaf_n, leaf_n)
        both = dot(rows_ref[...], factor).astype(BF16)
        for part in range(2):
            solved = both[part * half : (part + 1) * half]
            columns = pl.ds(part * leaf_n, leaf_n)
            for at in range(members):
                solved_ref[at, entry, :, columns] = solved[at * size : (at + 1) * size]
        for at, block in enumerate(group):
            copies.append(
                pltpu.make_async_copy(
                    solved_ref.at[at, entry], out_ref.at[own_pair ^ block, entry], sems.at[entry * members + at]
                )
            )
            copies[-1].start()
        for part in range(2):
            sums[part] += dot(member, both[part * half : (part + 1) * half, :sep_n])
    for part in range(2):
        columns = slice(part * sep_n, (part + 1) * sep_n)
        if code_ref is None:
            sums_ref[:, columns] = sums[part]
        else:
            total = sums[part] + before_ref[:, columns]
            keep_ref[:, columns] = total[: count // 2]
            send_ref[:, columns] = total[count // 2 :].astype(send_ref.dtype)
    if code_ref is not None:
        codes = jnp.where(here, code_ref[0, 0].astype(F32), 0.0)
        keep_ref[:, 2 * sep_n :] = codes[: count // 2]
        send_ref[:, 2 * sep_n :] = codes[count // 2 :].astype(send_ref.dtype)
    for copy in copies:
        copy.wait()


def tree_kernel(scales, keep_ref, arrived_ref, factors_ref, out_ref):
    sep_lib, sep_n = factors_ref.shape[0], factors_ref.shape[2]
    shots = out_ref.shape[0] // 2
    sums = keep_ref[...] + arrived_ref[...].astype(F32)
    above = jnp.zeros(out_ref.shape, F32)
    for level in reversed(range(len(scales))):
        here = sums[level * shots : (level + 1) * shots]
        code = jnp.max(here[0:1, 2 * sep_n :]).astype(jnp.int32) % sep_lib
        path = jnp.concatenate([here[:, :sep_n], here[:, sep_n : 2 * sep_n]], axis=0)
        operand = (path * scales[level] - above).astype(BF16)
        factor = factors_ref[code]
        by_re, by_im = dot(operand, factor[0]), dot(operand, factor[1])
        above = jnp.concatenate([by_re[:shots] - by_im[shots:], by_im[:shots] + by_re[shots:]], axis=0)
    out_ref[...] = above


def result_kernel(shots, pick_ref, above_ref, back_ref, out_ref, solved_ref, sems):
    leaves, _, width2 = out_ref.shape
    count = leaves * shots
    leaf_n = width2 // 2
    sep_n = above_ref.shape[1]
    shot = lax.broadcasted_iota(jnp.int32, (count, sep_n), 0) % shots
    copies = []
    for part in range(2):
        start = part * leaf_n
        solved = dot(pick_ref[...], back_ref[:, start : start + leaf_n])
        lifted = jnp.zeros((count, sep_n), F32)
        for at in range(shots):
            here = part * shots + at
            lifted = jnp.where(shot == at, above_ref[here : here + 1], lifted)
        solved = jnp.concatenate([solved[:, :sep_n] - lifted, solved[:, sep_n:]], axis=1).astype(BF16)
        columns = pl.ds(start, leaf_n)
        solved_ref[:, :, columns] = solved.reshape(leaves, shots, leaf_n)
        copies.append(
            pltpu.make_async_copy(solved_ref.at[:, :, columns], out_ref.at[:, :, columns], sems.at[part])
        )
        copies[part].start()
    for copy in copies:
        copy.wait()


def call(kernel, out_shape, args, smem=(), hbm=(), hbm_out=(), aliases={}, scratch=(), cost=None, limit=16):
    spaces = [pltpu.SMEM if at in smem else pltpu.HBM if at in hbm else VMEM for at in range(len(args))]
    shapes = out_shape if isinstance(out_shape, list) else [out_shape]
    out_specs = [pl.BlockSpec(memory_space=pltpu.HBM if at in hbm_out else VMEM) for at in range(len(shapes))]
    return pl.pallas_call(
        kernel,
        out_shape=out_shape,
        in_specs=[pl.BlockSpec(memory_space=space) for space in spaces],
        out_specs=out_specs if isinstance(out_shape, list) else out_specs[0],
        scratch_shapes=list(scratch),
        input_output_aliases=aliases,
        cost_estimate=cost and pl.CostEstimate(flops=cost[0], bytes_accessed=cost[1], transcendentals=0),
        compiler_params=pltpu.CompilerParams(vmem_limit_bytes=int(limit * 2**20)),
    )(*args)


def to_pairs(value):
    groups = [list(range(parity, lax.axis_size("leaf"), 2)) for parity in range(2)]
    return lax.all_to_all(value, "leaf", 0, 0, tiled=True, axis_index_groups=groups)


def path_sums(keep, send, shots, levels):
    bits = levels - 1
    sizes = [1 << bits - 1 - level for level in range(bits)] + [1]
    arrived = exchange(send, 1 << bits)
    for bit in range(-1, bits - 1):
        sums = keep + arrived.astype(F32)
        mine, other, start = [], [], 0
        for level, count in enumerate(sizes):
            for node in range(count):
                rows = sums[start * shots : (start + 1) * shots]
                start += 1
                if level > bit or bit < 0:
                    mine.append(rows)
                    other.append(rows)
                else:
                    (other if node % 2 else mine).append(rows)
            if level <= bit:
                sizes[level] //= 2
        keep = jnp.concatenate(mine)
        other = jnp.concatenate(other)
        arrived = exchange(other, 2 << bit) if bit >= 0 else exchange(other.astype(BF16), 1)
    return keep, arrived


def on_device(sources, transmission, media, sep_code, leaf_factors, sep_factors):
    leaves, shots, width2 = sources.shape[1:]
    leaf_n = width2 // 2
    front = transmission.shape[2] // 2
    sep_lib, sep_n = sep_factors.shape[0], sep_factors.shape[2]
    nleaf = lax.axis_size("leaf")
    levels = nleaf.bit_length() - 1
    capacity = max(2, leaves * 5 // (nleaf * 2))
    size = 2 * capacity * shots
    pairs = nleaf // 2
    slots = pairs * size
    source, tau = sources[0], transmission[0][:, None, :]
    own = leaf_factors[0]
    sibling = exchange(own, 1)

    face = jax.ShapeDtypeStruct((leaves, shots, 2 * front), BF16)
    rows = leaves * shots
    leaving = call(
        functools.partial(face_kernel, front),
        jax.ShapeDtypeStruct((rows, 2 * front), BF16),
        (source, tau),
        hbm=(0, 1),
        scratch=[VMEM(face.shape, BF16)] * 2 + [VMEM(tau.shape, F32), pltpu.SemaphoreType.DMA((3,))],
        limit=53.9,
    )
    arriving = around(leaving, "panel")
    tau_re, tau_im = tau[..., :front], tau[..., front:]
    for _ in range(lax.axis_size("panel") - 2):
        arriving = jnp.where(lax.axis_index("panel") > 0, arriving, 0).reshape(face.shape).astype(F32)
        real = arriving[..., :front] + source[..., leaf_n - front : leaf_n].astype(F32)
        imag = arriving[..., front:] + source[..., 2 * leaf_n - front :].astype(F32)
        leaving = jnp.concatenate([tau_re * real - tau_im * imag, tau_re * imag + tau_im * real], axis=-1)
        arriving = around(leaving.reshape(rows, 2 * front).astype(BF16), "panel")

    to_slots, from_slots = call(
        functools.partial(slot_kernel, shots, capacity),
        [jax.ShapeDtypeStruct((slots, rows), BF16), jax.ShapeDtypeStruct((rows, slots), BF16)],
        (media[0].reshape(1, leaves),),
    )
    block = jax.ShapeDtypeStruct((size, width2), BF16)
    sent = call(
        functools.partial(dispatch_kernel, front),
        [block] * pairs,
        (to_slots, source.reshape(rows, width2), arriving, sibling),
        hbm=(3,),
        scratch=[VMEM((rows, width2), BF16)],
    )
    far, near = list(range(pairs // 2, pairs)), list(range(1, pairs // 2))
    order = far[-1:] + near + far[-2::-1] + [0]
    arrived = {at: exchange(sent[at], 2 * at) if at else sent[at] for at in order}
    own, sibling = call(stage_kernel, [jax.ShapeDtypeStruct(own.shape, BF16)] * 2, (own, sibling, sent[0]), hbm=(2,))
    nodes = jax.ShapeDtypeStruct((pairs * shots, 2 * sep_n + LANES), F32)
    halves = (pairs, 2, size // 2, width2)
    first, last = order[: pairs // 2] + [0], order[pairs // 2 : -1]

    def scratch(group):
        return [
            VMEM((len(group) * size, width2), BF16),
            VMEM((len(group),) + halves[1:], BF16),
            pltpu.SemaphoreType.DMA((2 * len(group),)),
        ]

    solved, sums = call(
        functools.partial(leaf_kernel, shots, sep_n, first, pairs),
        [jax.ShapeDtypeStruct(halves, BF16), jax.ShapeDtypeStruct((2 * pairs * shots, 2 * sep_n), F32)],
        (own, sibling, *(arrived[at] for at in first)),
        hbm_out=(0,),
        scratch=scratch(first),
    )
    solved, keep, send = call(
        functools.partial(leaf_kernel, shots, sep_n, last, pairs),
        [jax.ShapeDtypeStruct(halves, BF16), nodes, nodes],
        (own, sibling, *(arrived[at] for at in last), sep_code % sep_lib, sums, solved),
        smem=(2 + len(last),),
        hbm=(4 + len(last),),
        hbm_out=(0,),
        aliases={4 + len(last): 0},
        scratch=scratch(last),
    )
    back = to_pairs(solved.reshape(pairs, size, width2)).reshape(slots, width2)
    keep, arrived = path_sums(keep, send, shots, levels)
    scales = [1.0 / math.sqrt(leaves * 2 ** (level + 1)) for level in range(levels)]
    above = call(
        functools.partial(tree_kernel, scales),
        jax.ShapeDtypeStruct((2 * shots, sep_n), F32),
        (keep, arrived, sep_factors),
        cost=(1, 1),
    )
    result = call(
        functools.partial(result_kernel, shots),
        jax.ShapeDtypeStruct((leaves, shots, width2), BF16),
        (from_slots, above, back),
        hbm_out=(0,),
        scratch=[VMEM((leaves, shots, width2), BF16), pltpu.SemaphoreType.DMA((2,))],
    )
    return result[None]


def solution(mesh):
    return jax.shard_map(
        on_device,
        mesh=mesh,
        in_specs=(
            P("panel", "leaf", None, None),
            P("panel", "leaf", None),
            P("panel", "leaf", None),
            P("panel", "leaf"),
            P("leaf", None, None, None),
            P(),
        ),
        out_specs=P("panel", "leaf", None, None),
        check_vma=False,
    )
```
